128 devices in a mesh: dp: 8 (over x_hi, y), comp: 16 (over x_lo, z, core).
Axes of the slice: x: 4 (x_hi: 2, x_lo: 2; x = x_hi * 2 + x_lo), y: 4, z: 4, core: 2. Of those that a mesh axis runs over, the one named last changes fastest.
Arguments:
- embeddings: bfloat16 [8192, 1024], P('dp', 'comp'), may hold values from -7 to 7
- means: bfloat16 [32768, 1024], P('comp'), may hold values from -3 to 3
- precisions: bfloat16 [32768, 1024], P('comp'), may hold values from 0.5 to 2
- log_weights: float32 [32768], P('comp'), may hold values from -4 to 4
- valid: int32 [8192], P('dp'), may hold values 0 or 1
Outputs:
- new_means: float32 [32768, 1024], P(('comp', 'dp'))
- new_vars: float32 [32768, 1024], P(('comp', 'dp'))
- new_weights: float32 [32768], P(('comp', 'dp'))
- mean_score: float32 [], replicated
The draws below stay inside these ranges and needn't reach their ends.
All inputs are finite; a program needn't handle non-finite values. No bound on the sum of `valid` on one device may be relied on, other than what follows from the above.
Results may differ from the reference program's by a relative error of at most 0.0022.
Values may be sent and summed in bfloat16 or wider, within the bound.
A program may use at most 128 MiB of HBM per device.

```python
import math
import jax
import jax.numpy as jnp
from jax import lax

D = 1024
K = 32768
ROWS = 8192


def draw_embeddings(key, part):
    key = jax.random.fold_in(key, 11)
    values = jnp.clip(jax.random.normal(key, (ROWS, D), jnp.float32), -6.0, 6.0)
    return values.astype(jnp.bfloat16)


def set_ends(result, key, smallest, top_value):
    shape = result.shape
    spot = [jax.random.randint(jax.random.fold_in(key, axis), (), 0, shape[axis]) for axis in range(len(shape))]
    result = result.at[tuple(spot)].set(smallest)
    longest = shape.index(max(shape))
    spot[longest] = (spot[longest] + 1) % shape[longest]
    return result.at[tuple(spot)].set(top_value)


def level_of(rng, dims, pieces, least, high):
    def one(dim, shards_of):
        heights = jax.random.uniform(jax.random.fold_in(jax.random.fold_in(rng, 6), dim), (shards_of,), jnp.float32, least / len(pieces), high / len(pieces))
        return jnp.repeat(jnp.exp(heights), dims[dim] // shards_of).reshape((-1,) + (1,) * (len(dims) - dim - 1))

    loudness = one(*pieces[0])
    for cut in pieces[1:]:
        loudness = loudness * one(*cut)
    return loudness


def noise(key, dims, deviation, most, shards=(), dtype=jnp.bfloat16):
    level = level_of(key, dims, shards, -0.22, 0.18) if shards else 1.0
    entries = jax.random.normal(key, dims, jnp.float32) * deviation * level
    return jnp.minimum(jnp.maximum(entries, -most), most).astype(dtype)


def setup_inputs(seed: int = 0) -> dict:
    keys = jax.random.split(jax.random.key(seed), 6)
    return {
        "embeddings": draw_embeddings(jax.random.fold_in(keys[5], 71), 0),
        "means": noise(keys[1], (K, D), 0.5, 3.0, ((0, 16),)),
        "precisions": jnp.clip(jnp.exp(math.log(2.0) - 1.3862944 * jax.random.uniform(keys[2], (K, D), jnp.float32) ** level_of(keys[2], (K, D), ((0, 16),), -0.2, 0.2)), 0.5, 2.0).astype(jnp.bfloat16),
        "log_weights": noise(keys[3], (K,), 1.0, 4.0, ((0, 16),), jnp.float32),
        "valid": set_ends((jax.random.randint(keys[4], (ROWS,), 0, 8) < 7).astype(jnp.int32), jax.random.fold_in(keys[4], 1), 0, 1),
    }


PRIOR_MASS = 1.0

def reference(embeddings, means, precisions, log_weights, valid):
    prec = precisions.astype(jnp.float32)
    centre = means.astype(jnp.float32)
    scaled = (prec * centre).astype(jnp.bfloat16)
    halfp = (0.5 * prec).astype(jnp.bfloat16)
    offset = log_weights + 0.5 * lax.optimization_barrier(jnp.sum(jnp.log(prec), axis=1)) - 0.5 * lax.optimization_barrier(jnp.sum(prec * centre * centre, axis=1))
    temper = 0.5 * math.sqrt(D)
    block = math.gcd(ROWS, 512)
    blocks = ROWS // block
    rows_in = embeddings.reshape(blocks, block, D)
    masks_in = valid.reshape(blocks, block)

    def advance(carry, items):
        first, second, weight_sum, score_sum, count = carry
        rows_now, mask_now = items
        wide = rows_now.astype(jnp.float32)
        squares = (wide * wide).astype(jnp.bfloat16)
        logits = (jnp.dot(rows_now, scaled.T, preferred_element_type=jnp.float32) - jnp.dot(squares, halfp.T, preferred_element_type=jnp.float32) + offset) / temper
        peak = lax.optimization_barrier(jnp.max(logits, axis=1))
        log_total = peak + jnp.log(lax.optimization_barrier(jnp.sum(jnp.exp(logits - peak[:, None]), axis=1)))
        maskf = mask_now.astype(jnp.float32)
        resp = (jnp.exp(logits - log_total[:, None]) * maskf[:, None]).astype(jnp.bfloat16)
        first = first + jnp.dot(resp.T, rows_now, preferred_element_type=jnp.float32)
        second = second + jnp.dot(resp.T, squares, preferred_element_type=jnp.float32)
        weight_sum = weight_sum + lax.optimization_barrier(jnp.sum(resp.astype(jnp.float32), axis=0))
        score_sum = score_sum + jnp.sum(maskf * log_total)
        count = count + jnp.sum(maskf)
        return ((first, second, weight_sum, score_sum, count), None)
    start = (jnp.zeros((K, D), jnp.float32), jnp.zeros((K, D), jnp.float32), jnp.zeros((K,), jnp.float32), jnp.zeros((), jnp.float32), jnp.zeros((), jnp.float32))
    (first, second, weight_sum, score_sum, count), _ = lax.scan(advance, start, (rows_in, masks_in))
    count = jnp.maximum(count, 1.0)
    denom = weight_sum + PRIOR_MASS
    new_means = (first + PRIOR_MASS * centre) / denom[:, None]
    new_vars = (second + PRIOR_MASS * (1.0 / prec + centre * centre)) / denom[:, None] - new_means * new_means
    return (new_means, new_vars, weight_sum / count, score_sum / count)
```

```python
import math

import jax
import jax.numpy as jnp
from jax import lax
from jax.sharding import PartitionSpec as P
import jax.experimental.pallas as pl
import jax.experimental.pallas.tpu as pltpu

PRIOR_MASS = 1.0
MESH = pl.DeviceIdType.MESH
F32, BF16 = jnp.float32, jnp.bfloat16

LOW, MID, TOP = 0, 128, 320
Q = 32
H = 96
CHUNKS = 8
LANES = 128
CONTRACT_LAST = (((1,), (1,)), ((), ()))
CONTRACT = (((1,), (0,)), ((), ()))


def kernel(emb_hbm, means_hbm, prec_hbm, lw_ref, valid_ref,
           out_means, out_vars, out_weights, out_score,
           emb, means, prec, give, take, grid, weights, offsets, valids, masks,
           squares, expo, peaks, stat_a, stat_b, resp, moments, mass, got_moments, got_mass, score_mine, score_got, score_acc,
           load_sem, send_one, recv_one, send_hop, recv_hop, send_fwd, recv_fwd, send_a, recv_a, send_b, recv_b):
    dp, comp = lax.axis_index("dp"), lax.axis_index("comp")
    xh, y = dp // 4, dp % 4
    xl, z, core = comp // 8, (comp // 2) % 4, comp % 2
    x = xh * 2 + xl
    temper = 0.5 * math.sqrt(1024)

    def dev(x, y, z, core):
        return ((x // 2) * 4 + y, (x % 2) * 8 + z * 2 + core)

    def along(axis, step):
        if axis == "x":
            return dev((x + step) % 4, y, z, core)
        if axis == "y":
            return dev(x, (y + step) % 4, z, core)
        return dev(x, y, (z + step) % 4, core)

    sibling = dev(x, y, z, 1 - core)
    slot_a = x * 2 + y % 2
    slot_b = z * 2 + y // 2

    def peer_a(k):
        to = (slot_a + k) % 8
        return dev(to // 2, (y // 2) * 2 + to % 2, z, core)

    def peer_b(k):
        to = (slot_b + k) % 8
        return dev(x, (to % 2) * 2 + y % 2, to // 2, core)

    def push(ref, to, ssem, rsem, dst=None):
        pltpu.make_async_remote_copy(
            src_ref=ref, dst_ref=ref if dst is None else dst, send_sem=ssem, recv_sem=rsem, device_id=to, device_id_type=MESH
        ).start()

    def arrived(ref, rsem):
        pltpu.make_async_remote_copy(
            src_ref=ref, dst_ref=ref, send_sem=send_one.at[0], recv_sem=rsem, device_id=sibling, device_id_type=MESH
        ).wait_recv()

    def sent(ref, ssem):
        pltpu.make_async_remote_copy(
            src_ref=ref, dst_ref=ref, send_sem=ssem, recv_sem=recv_one.at[0], device_id=sibling, device_id_type=MESH
        ).wait_send()

    own = pl.multiple_of(dp * 256, 256)
    load_emb = pltpu.make_async_copy(emb_hbm, emb, load_sem.at[0])
    load_means = pltpu.make_async_copy(means_hbm.at[pl.ds(own, 256)], means, load_sem.at[1])
    load_prec = pltpu.make_async_copy(prec_hbm.at[pl.ds(own, 256)], prec, load_sem.at[2])
    load_emb.start()
    load_means.start()
    load_prec.start()

    barrier = pltpu.get_barrier_semaphore()
    friends = [sibling]
    for k in range(1, 4):
        friends += [along("x", k), along("y", k), along("z", k)]
        friends += []
    for k in range(4):
        if k:
            friends.append(dev((x + k) % 4, (y // 2) * 2 + 1 - y % 2, z, core))
            friends.append(dev(x, (y + 2) % 4, (z + k) % 4, core))
    for friend in friends:
        pl.semaphore_signal(barrier, inc=1, device_id=friend, device_id_type=MESH)
    load_emb.wait()
    pl.semaphore_wait(barrier, len(friends))

    low, high = emb[0:512, :], emb[512:1024, :]
    keep = jnp.where(core == 0, low, high)
    part = jnp.where(core == 0, high, low)
    give[...] = jnp.concatenate([part, part], axis=1)
    push(give, sibling, send_one.at[0], recv_one.at[0], dst=take)
    vrow = jnp.where(core == 0, valid_ref[0:4, :], valid_ref[4:8, :]).astype(F32)
    valids[xh, y] = jnp.concatenate([vrow, vrow], axis=0)
    for k in range(1, 4):
        push(valids.at[xh, y], along("y", k), send_one.at[9], recv_one.at[9])
    arrived(take, recv_one.at[0])
    mine = lax.broadcasted_iota(jnp.int32, (512, LANES), 1) // 64 == core
    shard = jnp.where(mine, jnp.concatenate([keep, keep], axis=1), take[...])
    for q in range(4):
        grid[xh, q, xl, z, pl.ds(pl.multiple_of(y * Q, Q), Q), :] = shard[q * Q:(q + 1) * Q]
    grid[xh, y, xl, z, MID:TOP, :] = shard[MID:TOP]
    low_h = pl.multiple_of(TOP + xh * H, 32)
    for h in range(2):
        grid[y // 2, (y % 2) * 2 + h, xl, z, pl.ds(low_h, H), :] = shard[TOP + h * H:TOP + (h + 1) * H]

    low_q = pl.multiple_of(y * Q, Q)
    first = (
        ("z", grid.at[xh, :, xl, z, pl.ds(low_q, Q)]),
        ("x", grid.at[xh, y, xl, z, pl.ds(MID, TOP - MID)]),
        ("y", grid.at[y // 2, pl.ds((y % 2) * 2, 2), xl, z, pl.ds(low_h, H)]),
    )
    for k in range(1, 4):
        for part_no, (axis, ref) in enumerate(first):
            push(ref, along(axis, k), send_one.at[1 + part_no], recv_one.at[1 + part_no])

    load_means.wait()
    load_prec.wait()
    for tile in range(2):
        row = jnp.broadcast_to(lw_ref[pl.ds(dp * 2 + tile, 1), :], (LANES, LANES))
        offsets[1, tile * LANES:(tile + 1) * LANES, :] = jnp.transpose(row)

    @pl.loop(0, 8)
    def _(t):
        rows = pl.ds(pl.multiple_of(t * 32, 32), 32)
        p = prec[rows, :].astype(F32)
        c = means[rows, :].astype(F32)
        scaled = (p * c).astype(BF16).astype(F32)
        halfp = (0.5 * p).astype(BF16).astype(F32)
        weights[1, rows, 0:1024] = (scaled * (1.0 / temper)).astype(BF16)
        weights[1, rows, 1024:2048] = (halfp * (-1.0 / temper)).astype(BF16)
        both = 0.5 * jnp.sum(jnp.log(p), axis=1, keepdims=True) - 0.5 * jnp.sum(p * c * c, axis=1, keepdims=True)
        offsets[1, rows, :] = (offsets[1, rows, :] + both) * (1.0 / temper)

    push(weights.at[1], sibling, send_one.at[7], recv_one.at[7], dst=weights.at[0])
    push(offsets.at[1], sibling, send_one.at[8], recv_one.at[8], dst=offsets.at[0])

    first_done = (grid.at[0, 0, 0, 0, pl.ds(0, 384)], grid.at[0, 0, 0, pl.ds(0, 3), pl.ds(0, 192)], grid.at[0, 0, 0, pl.ds(0, 3), pl.ds(0, 192)])
    second = (
        ("x", grid.at[xh, :, xl, :, pl.ds(low_q, Q)]),
        ("y", grid.at[:, y, :, z, pl.ds(MID, TOP - MID)]),
        ("z", grid.at[:, :, xl, z, pl.ds(low_h, H)]),
    )
    for part_no, (axis, ref) in enumerate(second):
        arrived(first_done[part_no], recv_one.at[1 + part_no])
        for k in range(1, 4):
            push(ref, along(axis, k), send_one.at[4 + part_no], recv_one.at[4 + part_no])
    arrived(valids.at[0, pl.ds(0, 3)], recv_one.at[9])
    push(valids.at[xh], along("x", 2), send_one.at[10], recv_one.at[10])

    moments[...] = jnp.zeros_like(moments)
    mass[...] = jnp.zeros_like(mass)
    score_acc[...] = jnp.zeros_like(score_acc)

    second_done = (grid.at[0, 0, 0, pl.ds(0, 3)], grid.at[0, pl.ds(0, 3), 0, :, pl.ds(0, 192)], grid.at[0, pl.ds(0, 3), 0, :, pl.ds(0, 192)])
    for part_no in range(3):
        arrived(second_done[part_no], recv_one.at[4 + part_no])

    def third(i, j, step):
        yy, zz, xx = (y + step) % 4, (z + step) % 4, (x + step) % 4
        return (
            ("y", grid.at[i, j, :, :, pl.ds(pl.multiple_of(yy * Q, Q), Q)]),
            ("z", grid.at[i, j, :, zz, pl.ds(MID, TOP - MID)]),
            ("x", grid.at[i, j, xx % 2, :, pl.ds(pl.multiple_of(TOP + (xx // 2) * H, 32), H)]),
        )

    @pl.loop(0, CHUNKS)
    def _(s):
        for axis, ref in third(s // 4, s % 4, 0):
            for step in (1, 3):
                push(ref, along(axis, step), send_hop.at[s], recv_hop.at[s])

    arrived(valids.at[0], recv_one.at[10])
    place = lax.broadcasted_iota(jnp.int32, (8, 512), 1)

    def lanes_of(block):
        v = valids[block // 4, block % 4]
        return jnp.broadcast_to(jnp.concatenate([v[i:i + 1, :] for i in range(4)], axis=1), (8, 512))

    by_block = [lanes_of(b) for b in range(8)]
    count_plane = functools_sum([jnp.sum(b[0:1, :], axis=1, keepdims=True) for b in by_block])
    for s in range(CHUNKS):
        q, h = s % 4, s % 2
        out = by_block[s]
        for yy in range(4):
            moved = pltpu.roll(by_block[(s // 4) * 4 + yy], ((yy - q) * Q) % 512, 1)
            out = jnp.where((place >= yy * Q) & (place < (yy + 1) * Q), moved, out)
        for xx in range(2):
            moved = pltpu.roll(by_block[xx * 4 + s // 2], ((xx - h) * H) % 512, 1)
            out = jnp.where((place >= TOP + xx * H) & (place < TOP + (xx + 1) * H), moved, out)
        masks[s] = out

    arrived(weights.at[0], recv_one.at[7])
    arrived(offsets.at[0], recv_one.at[8])

    def logits_of(s):
        i, j, slot = s // 4, s % 4, s % 4
        tops, sums = [], []
        for n in range(2):
            rows = pl.ds(n * 256, 256)
            xs = jnp.concatenate([grid[i, j, f // 4, f % 4, rows, :] for f in range(8)], axis=1)
            wide = xs.astype(F32)
            sq = (wide * wide).astype(BF16)
            squares[slot, rows, :] = sq
            w = weights[...].reshape(512, 2048)
            l = lax.dot_general(w[:, 0:1024], xs, CONTRACT_LAST, preferred_element_type=F32)
            l = l + lax.dot_general(w[:, 1024:2048], sq, CONTRACT_LAST, preferred_element_type=F32)
            off = offsets[...].reshape(512, LANES)
            l = l + jnp.concatenate([off, off], axis=1)
            top = jnp.max(l, axis=0, keepdims=True)
            e = jnp.exp(l - top)
            expo[slot, :, rows] = e
            total = jnp.sum(e, axis=0, keepdims=True)
            tops += [top[:, 0:128], top[:, 128:256]]
            sums += [total[:, 0:128], total[:, 128:256]]
        stat = jnp.concatenate(tops + sums, axis=0)
        stat_a[s, slot_a] = stat
        peaks[slot] = stat

    def combine(ref):
        both = [ref[k] for k in range(8)]
        top = both[0][0:4]
        for b in both[1:]:
            top = jnp.maximum(top, b[0:4])
        total = jnp.zeros_like(top)
        for b in both:
            total = total + b[4:8] * jnp.exp(b[0:4] - top)
        return top, total

    def moments_of(s, weight):
        i, j, slot = s // 4, s % 4, s % 4
        for half in range(2):
            for part in range(2):
                r = (expo[slot, pl.ds(half * 256 + part * 128, 128), :] * weight).astype(BF16)
                resp[pl.ds(part * 128, 128), :] = r
                wide = r.astype(F32)
                mass[half, pl.ds(part * 128, 128), :] += wide[:, 0:128] + wide[:, 128:256] + wide[:, 256:384] + wide[:, 384:512]
            r = resp[...]
            for n in range(4):
                xs = jnp.concatenate([grid[i, j, (2 * n) // 4, (2 * n) % 4], grid[i, j, (2 * n + 1) // 4, (2 * n + 1) % 4]], axis=1)
                moments[half, :, n * 256:(n + 1) * 256] += lax.dot_general(r, xs, CONTRACT, preferred_element_type=F32)
            for n in range(4):
                sq = squares[slot, :, n * 256:(n + 1) * 256]
                moments[half, :, 1024 + n * 256:1024 + (n + 1) * 256] += lax.dot_general(r, sq, CONTRACT, preferred_element_type=F32)
            if half == 0:
                @pl.when(s == CHUNKS - 1)
                def _():
                    push(moments.at[0], sibling, send_one.at[11], recv_one.at[11], dst=got_moments)
                    push(mass.at[0], sibling, send_one.at[12], recv_one.at[12], dst=got_mass)

    @pl.loop(0, CHUNKS + 3)
    def _(it):
        @pl.when(it < CHUNKS)
        def _():
            s = it
            i, j = s // 4, s % 4
            arrived(grid.at[0, 0, 0], recv_hop.at[s])
            step = 1 - 2 * (s % 2)
            for axis, ref in third(i, j, 4 - step):
                push(ref, along(axis, 4 + step), send_fwd.at[s], recv_fwd.at[s])

        @pl.when((it >= 1) & (it < CHUNKS + 1))
        def _():
            s = it - 1
            arrived(grid.at[0, 0, 0, pl.ds(0, 2)], recv_fwd.at[s])
            logits_of(s)
            for k in range(1, 8):
                push(stat_a.at[s, slot_a], peer_a(k), send_a.at[s], recv_a.at[s])

        @pl.when((it >= 2) & (it < CHUNKS + 2))
        def _():
            s = it - 2
            arrived(stat_a.at[s, pl.ds(0, 7)], recv_a.at[s])
            top, total = combine(stat_a.at[s])
            stat_b[s, slot_b] = jnp.concatenate([top, total], axis=0)
            for k in range(1, 8):
                push(stat_b.at[s, slot_b], peer_b(k), send_b.at[s], recv_b.at[s])

        @pl.when(it >= 3)
        def _():
            s = it - 3
            arrived(stat_b.at[s, pl.ds(0, 7)], recv_b.at[s])
            top, total = combine(stat_b.at[s])
            log_total = top + jnp.log(total)
            mask = masks[s][0:1, :]
            scale = jnp.exp(peaks[s % 4][0:4] - log_total)
            scale = jnp.concatenate([scale[k:k + 1, :] for k in range(4)], axis=1) * mask
            score = jnp.concatenate([log_total[k:k + 1, :] for k in range(4)], axis=1) * mask
            score_acc[0:1, :] += score
            moments_of(s, scale)

    score_plane = jnp.sum(score_acc[0:1, :], axis=1, keepdims=True)
    score_mine[...] = jnp.concatenate([jnp.broadcast_to(score_plane, (4, LANES)), jnp.broadcast_to(count_plane, (4, LANES))], axis=0)
    push(score_mine, sibling, send_one.at[13], recv_one.at[13], dst=score_got)
    arrived(score_got, recv_one.at[13])
    both = score_mine[...] + score_got[...]
    count = jnp.maximum(both[4:5, 0:1], 1.0)
    out_score[...] = both[0:1, :] / count
    arrived(got_mass, recv_one.at[12])
    arrived(got_moments, recv_one.at[11])

    @pl.loop(0, 8)
    def _(t):
        rows = pl.ds(pl.multiple_of(t * 32, 32), 32)
        weight = jnp.sum(mass[1, rows, :] + got_mass[rows, :], axis=1, keepdims=True)
        got_mass[rows, :] = jnp.broadcast_to(weight, (32, LANES))
        scale = 1.0 / (weight + PRIOR_MASS)
        c = means[rows, :].astype(F32)
        p = prec[rows, :].astype(F32)
        m = (moments[1, rows, 0:1024] + got_moments[rows, 0:1024] + PRIOR_MASS * c) * scale
        out_means[rows, :] = m
        out_vars[rows, :] = (moments[1, rows, 1024:2048] + got_moments[rows, 1024:2048] + PRIOR_MASS * (1.0 / p + c * c)) * scale - m * m

    for tile in range(2):
        out_weights[tile:tile + 1, :] = jnp.transpose(got_mass[tile * LANES:(tile + 1) * LANES, :])[0:1, :] / count

    sent(give, send_one.at[0])
    for part_no in range(3):
        sent(first_done[part_no], send_one.at[1 + part_no])
        sent(second_done[part_no], send_one.at[4 + part_no])
    sent(weights.at[1], send_one.at[7])
    sent(offsets.at[1], send_one.at[8])
    sent(valids.at[0, pl.ds(0, 3)], send_one.at[9])
    sent(valids.at[0], send_one.at[10])
    sent(moments.at[0], send_one.at[11])
    sent(mass.at[0], send_one.at[12])
    sent(score_mine, send_one.at[13])

    @pl.loop(0, CHUNKS)
    def _(s):
        sent(grid.at[0, 0, 0], send_hop.at[s])
        sent(grid.at[0, 0, 0, pl.ds(0, 2)], send_fwd.at[s])
        sent(stat_a.at[s, pl.ds(0, 7)], send_a.at[s])
        sent(stat_b.at[s, pl.ds(0, 7)], send_b.at[s])


def functools_sum(items):
    total = items[0]
    for item in items[1:]:
        total = total + item
    return total


def per_device(embeddings, means, precisions, log_weights, valid):
    hbm = pl.BlockSpec(memory_space=pl.ANY)
    vmem = pl.BlockSpec(memory_space=pltpu.VMEM)
    dma = pltpu.SemaphoreType.DMA
    new_means, new_vars, weights, score = pl.pallas_call(
        kernel,
        out_shape=(
            jax.ShapeDtypeStruct((256, 1024), F32),
            jax.ShapeDtypeStruct((256, 1024), F32),
            jax.ShapeDtypeStruct((2, LANES), F32),
            jax.ShapeDtypeStruct((1, LANES), F32),
        ),
        in_specs=[hbm, hbm, hbm, vmem, vmem],
        out_specs=[vmem] * 4,
        scratch_shapes=[
            pltpu.VMEM((1024, 64), BF16),
            pltpu.VMEM((256, 1024), BF16),
            pltpu.VMEM((256, 1024), BF16),
            pltpu.VMEM((512, LANES), BF16),
            pltpu.VMEM((512, LANES), BF16),
            pltpu.VMEM((2, 4, 2, 4, 512, LANES), BF16),
            pltpu.VMEM((2, 256, 2048), BF16),
            pltpu.VMEM((2, 256, LANES), F32),
            pltpu.VMEM((2, 4, 8, LANES), F32),
            pltpu.VMEM((CHUNKS, 8, 512), F32),
            pltpu.VMEM((4, 512, 1024), BF16),
            pltpu.VMEM((4, 512, 512), F32),
            pltpu.VMEM((4, 8, LANES), F32),
            pltpu.VMEM((CHUNKS, 8, 8, LANES), F32),
            pltpu.VMEM((CHUNKS, 8, 8, LANES), F32),
            pltpu.VMEM((256, 512), BF16),
            pltpu.VMEM((2, 256, 2048), F32),
            pltpu.VMEM((2, 256, LANES), F32),
            pltpu.VMEM((256, 2048), F32),
            pltpu.VMEM((256, LANES), F32),
            pltpu.VMEM((8, LANES), F32),
            pltpu.VMEM((8, LANES), F32),
            pltpu.VMEM((8, 512), F32),
            dma((3,)),
            dma((14,)), dma((14,)),
            dma((CHUNKS,)), dma((CHUNKS,)),
            dma((CHUNKS,)), dma((CHUNKS,)),
            dma((CHUNKS,)), dma((CHUNKS,)),
            dma((CHUNKS,)), dma((CHUNKS,)),
        ],
        compiler_params=pltpu.CompilerParams(
            collective_id=0, has_side_effects=True, vmem_limit_bytes=56 << 20
        ),
        cost_estimate=pl.CostEstimate(flops=17 << 30, bytes_accessed=8 << 20, transcendentals=4 << 20),
        name="mixture_step",
    )(embeddings, means, precisions, log_weights.reshape(16, LANES), valid.reshape(8, LANES))
    return new_means, new_vars, weights.reshape(256), score[0, 0]


def solution(mesh):
    in_specs = (P("dp", "comp"), P("comp", None), P("comp", None), P("comp"), P("dp"))
    out_specs = (P(("comp", "dp"), None), P(("comp", "dp"), None), P(("comp", "dp")), P())
    return jax.shard_map(
        per_device, mesh=mesh, in_specs=in_specs, out_specs=out_specs, check_vma=False
    )
```

```python
import math

import jax
import jax.numpy as jnp
from jax import lax
from jax.sharding import PartitionSpec as P
import jax.experimental.pallas as pl
import jax.experimental.pallas.tpu as pltpu

PRIOR_MASS = 1.0
MESH = pl.DeviceIdType.MESH
F32, BF16 = jnp.float32, jnp.bfloat16

LOW, MID, TOP = 0, 128, 320
Q = 32
H = 96
CHUNKS = 8
AHEAD = 3
LAG_L, LAG_A, LAG_M = 2, 4, 6
LANES = 128
CONTRACT_LAST = (((1,), (1,)), ((), ()))
CONTRACT = (((1,), (0,)), ((), ()))


def kernel(emb_hbm, means_hbm, prec_hbm, lw_hbm, valid_hbm,
           moments, got_moments, mass, got_mass, means, prec, score_mine, score_got,
           emb, lw_ref, valid_ref, take, grid, weights, offsets, valids, masks,
           squares, expo, peaks, stat_a, stat_b, resp, far_rows, far_expo, scales, far_scale, score_acc,
           load_sem, send_one, recv_one, send_hop, recv_hop, send_fwd, recv_fwd, send_a, recv_a, send_b, recv_b):
    dp, comp = lax.axis_index("dp"), lax.axis_index("comp")
    xh, y = dp // 4, dp % 4
    xl, z, core = comp // 8, (comp // 2) % 4, comp % 2
    x = xh * 2 + xl
    temper = 0.5 * math.sqrt(1024)

    def dev(x, y, z, core):
        return ((x // 2) * 4 + y, (x % 2) * 8 + z * 2 + core)

    def along(axis, step):
        if axis == "x":
            return dev((x + step) % 4, y, z, core)
        if axis == "y":
            return dev(x, (y + step) % 4, z, core)
        return dev(x, y, (z + step) % 4, core)

    sibling = dev(x, y, z, 1 - core)
    slot_a = x * 2 + y % 2
    slot_b = z * 2 + y // 2

    def peer_a(k):
        to = (slot_a + k) % 8
        return dev(to // 2, (y // 2) * 2 + to % 2, z, core)

    def peer_b(k):
        to = (slot_b + k) % 8
        return dev(x, (to % 2) * 2 + y % 2, to // 2, core)

    def push(ref, to, ssem, rsem, dst=None):
        pltpu.make_async_remote_copy(
            src_ref=ref, dst_ref=ref if dst is None else dst, send_sem=ssem, recv_sem=rsem, device_id=to, device_id_type=MESH
        ).start()

    def arrived(ref, rsem):
        pltpu.make_async_remote_copy(
            src_ref=ref, dst_ref=ref, send_sem=send_one.at[0], recv_sem=rsem, device_id=sibling, device_id_type=MESH
        ).wait_recv()

    def sent(ref, ssem):
        pltpu.make_async_remote_copy(
            src_ref=ref, dst_ref=ref, send_sem=ssem, recv_sem=recv_one.at[0], device_id=sibling, device_id_type=MESH
        ).wait_send()

    own = pl.multiple_of(dp * 256, 256)
    load_emb = pltpu.make_async_copy(emb_hbm.at[:, pl.ds(pl.multiple_of(core * 512, 512), 512)], emb, load_sem.at[0])
    load_means = pltpu.make_async_copy(means_hbm.at[pl.ds(own, 256)], means, load_sem.at[1])
    load_prec = pltpu.make_async_copy(prec_hbm.at[pl.ds(own, 256)], prec, load_sem.at[2])
    load_lw = pltpu.make_async_copy(lw_hbm, lw_ref, load_sem.at[3])
    load_valid = pltpu.make_async_copy(valid_hbm, valid_ref, load_sem.at[4])
    load_emb.start()
    load_valid.start()
    load_lw.start()
    load_means.start()
    load_prec.start()

    barrier = pltpu.get_barrier_semaphore()
    friends = [sibling]
    for k in range(1, 4):
        friends += [along("x", k), along("y", k), along("z", k)]
        friends += []
    for k in range(4):
        if k:
            friends.append(dev((x + k) % 4, (y // 2) * 2 + 1 - y % 2, z, core))
            friends.append(dev(x, (y + 2) % 4, (z + k) % 4, core))
    for friend in friends:
        pl.semaphore_signal(barrier, inc=1, device_id=friend, device_id_type=MESH)
    pl.semaphore_wait(barrier, len(friends))

    give = emb_hbm.at[:, pl.ds(pl.multiple_of((1 - core) * 512, 512), 512)]
    push(give, sibling, send_one.at[0], recv_one.at[0], dst=take)
    load_valid.wait()
    vrow = jnp.where(core == 0, valid_ref[0:4, :], valid_ref[4:8, :]).astype(F32)
    valids[xh, y] = jnp.concatenate([vrow, vrow], axis=0)
    for k in range(1, 4):
        push(valids.at[xh, y], along("y", k), send_one.at[9], recv_one.at[9])
    load_emb.wait()
    arrived(take, recv_one.at[0])
    kept, taken = emb[...], take[...]
    shard = jnp.concatenate([jnp.where(core == 0, kept, taken), jnp.where(core == 0, taken, kept)], axis=0)
    shard = jnp.transpose(shard)
    for q in range(4):
        grid[xh, q, xl, z, pl.ds(pl.multiple_of(y * Q, Q), Q), :] = shard[q * Q:(q + 1) * Q]
    grid[xh, y, xl, z, MID:TOP, :] = shard[MID:TOP]
    low_h = pl.multiple_of(TOP + xh * H, 32)
    for h in range(2):
        grid[y // 2, (y % 2) * 2 + h, xl, z, pl.ds(low_h, H), :] = shard[TOP + h * H:TOP + (h + 1) * H]

    low_q = pl.multiple_of(y * Q, Q)
    first = (
        ("z", grid.at[xh, :, xl, z, pl.ds(low_q, Q)]),
        ("x", grid.at[xh, y, xl, z, pl.ds(MID, TOP - MID)]),
        ("y", grid.at[y // 2, pl.ds((y % 2) * 2, 2), xl, z, pl.ds(low_h, H)]),
    )
    for k in range(1, 4):
        for part_no, (axis, ref) in enumerate(first):
            push(ref, along(axis, k), send_one.at[1 + part_no], recv_one.at[1 + part_no])

    load_means.wait()
    load_prec.wait()
    load_lw.wait()
    for tile in range(2):
        row = jnp.broadcast_to(lw_ref[pl.ds(dp * 2 + tile, 1), :], (LANES, LANES))
        offsets[1, tile * LANES:(tile + 1) * LANES, :] = jnp.transpose(row)

    @pl.loop(0, 8)
    def _(t):
        rows = pl.ds(pl.multiple_of(t * 32, 32), 32)
        p = prec[rows, :].astype(F32)
        c = means[rows, :].astype(F32)
        scaled = (p * c).astype(BF16).astype(F32)
        halfp = (0.5 * p).astype(BF16).astype(F32)
        weights[1, rows, 0:1024] = (scaled * (1.0 / temper)).astype(BF16)
        weights[1, rows, 1024:2048] = (halfp * (-1.0 / temper)).astype(BF16)
        both = 0.5 * jnp.sum(jnp.log(p), axis=1, keepdims=True) - 0.5 * jnp.sum(p * c * c, axis=1, keepdims=True)
        offsets[1, rows, :] = (offsets[1, rows, :] + both) * (1.0 / temper)

    push(weights.at[1], sibling, send_one.at[7], recv_one.at[7], dst=weights.at[0])
    push(offsets.at[1], sibling, send_one.at[8], recv_one.at[8], dst=offsets.at[0])

    first_done = (grid.at[0, 0, 0, 0, pl.ds(0, 384)], grid.at[0, 0, 0, pl.ds(0, 3), pl.ds(0, 192)], grid.at[0, 0, 0, pl.ds(0, 3), pl.ds(0, 192)])
    second = (
        ("x", grid.at[xh, :, xl, :, pl.ds(low_q, Q)]),
        ("y", grid.at[:, y, :, z, pl.ds(MID, TOP - MID)]),
        ("z", grid.at[:, :, xl, z, pl.ds(low_h, H)]),
    )
    for part_no, (axis, ref) in enumerate(second):
        arrived(first_done[part_no], recv_one.at[1 + part_no])
        for k in range(1, 4):
            push(ref, along(axis, k), send_one.at[4 + part_no], recv_one.at[4 + part_no])
    arrived(valids.at[0, pl.ds(0, 3)], recv_one.at[9])
    push(valids.at[xh], along("x", 2), send_one.at[10], recv_one.at[10])

    moments[...] = jnp.zeros_like(moments)
    mass[...] = jnp.zeros_like(mass)
    score_acc[...] = jnp.zeros_like(score_acc)

    second_done = (grid.at[0, 0, 0, pl.ds(0, 3)], grid.at[0, pl.ds(0, 3), 0, :, pl.ds(0, 192)], grid.at[0, pl.ds(0, 3), 0, :, pl.ds(0, 192)])
    for part_no in range(3):
        arrived(second_done[part_no], recv_one.at[4 + part_no])

    def third(i, j, step):
        yy, zz, xx = (y + step) % 4, (z + step) % 4, (x + step) % 4
        return (
            ("y", grid.at[i, j, :, :, pl.ds(pl.multiple_of(yy * Q, Q), Q)]),
            ("z", grid.at[i, j, :, zz, pl.ds(MID, TOP - MID)]),
            ("x", grid.at[i, j, xx % 2, :, pl.ds(pl.multiple_of(TOP + (xx // 2) * H, 32), H)]),
        )

    def hop(s):
        for axis, ref in third(s // 4, s % 4, 0):
            for step in (1, 3):
                push(ref, along(axis, step), send_hop.at[s], recv_hop.at[s])

    @pl.loop(0, AHEAD)
    def _(s):
        hop(s)

    arrived(valids.at[0], recv_one.at[10])
    place = lax.broadcasted_iota(jnp.int32, (8, 512), 1)

    def lanes_of(block):
        v = valids[block // 4, block % 4]
        return jnp.broadcast_to(jnp.concatenate([v[i:i + 1, :] for i in range(4)], axis=1), (8, 512))

    by_block = [lanes_of(b) for b in range(8)]
    count_plane = functools_sum([jnp.sum(b[0:1, :], axis=1, keepdims=True) for b in by_block])
    for s in range(CHUNKS):
        q, h = s % 4, s % 2
        out = by_block[s]
        for yy in range(4):
            moved = pltpu.roll(by_block[(s // 4) * 4 + yy], ((yy - q) * Q) % 512, 1)
            out = jnp.where((place >= yy * Q) & (place < (yy + 1) * Q), moved, out)
        for xx in range(2):
            moved = pltpu.roll(by_block[xx * 4 + s // 2], ((xx - h) * H) % 512, 1)
            out = jnp.where((place >= TOP + xx * H) & (place < TOP + (xx + 1) * H), moved, out)
        masks[s] = out

    arrived(weights.at[0], recv_one.at[7])
    arrived(offsets.at[0], recv_one.at[8])

    def logits_of(s):
        i, j, slot = s // 4, s % 4, s
        tops, sums = [], []
        for n in range(2):
            rows = pl.ds(n * 256, 256)
            xs = jnp.concatenate([grid[i, j, f // 4, f % 4, rows, :] for f in range(8)], axis=1)
            wide = xs.astype(F32)
            sq = (wide * wide).astype(BF16)
            squares[slot, rows, :] = sq
            w = weights[...].reshape(512, 2048)
            l = lax.dot_general(w[:, 0:1024], xs, CONTRACT_LAST, preferred_element_type=F32)
            l = l + lax.dot_general(w[:, 1024:2048], sq, CONTRACT_LAST, preferred_element_type=F32)
            off = offsets[...].reshape(512, LANES)
            l = l + jnp.concatenate([off, off], axis=1)
            top = jnp.max(l, axis=0, keepdims=True)
            e = jnp.exp(l - top)
            expo[slot, :, rows] = e
            total = jnp.sum(e, axis=0, keepdims=True)
            tops += [top[:, 0:128], top[:, 128:256]]
            sums += [total[:, 0:128], total[:, 128:256]]
        stat = jnp.concatenate(tops + sums, axis=0)
        stat_a[s, slot_a] = stat
        peaks[slot] = stat

    def combine(ref):
        both = [ref[k] for k in range(8)]
        top = both[0][0:4]
        for b in both[1:]:
            top = jnp.maximum(top, b[0:4])
        total = jnp.zeros_like(top)
        for b in both:
            total = total + b[4:8] * jnp.exp(b[0:4] - top)
        return top, total

    def add_half(half, e_ref, row0, weight, features, squared):
        for part in range(2):
            r = (e_ref[pl.ds(row0 + part * 128, 128), :] * weight).astype(BF16)
            resp[pl.ds(part * 128, 128), :] = r
            wide = r.astype(F32)
            mass[half, pl.ds(part * 128, 128), :] += wide[:, 0:128] + wide[:, 128:256] + wide[:, 256:384] + wide[:, 384:512]
        r = resp[...]
        for n in range(4):
            xs = jnp.concatenate([features(2 * n), features(2 * n + 1)], axis=1)
            moments[half, :, n * 256:(n + 1) * 256] += lax.dot_general(r, xs, CONTRACT, preferred_element_type=F32)
            sq = squared(n, xs)
            moments[half, :, 1024 + n * 256:1024 + (n + 1) * 256] += lax.dot_general(r, sq, CONTRACT, preferred_element_type=F32)

    def moments_of(s, weight):
        i, j = s // 4, s % 4

        def features(f):
            return grid[i, j, f // 4, f % 4]

        def squared(n, xs):
            return squares[s, :, n * 256:(n + 1) * 256]

        @pl.when(s < CHUNKS - 1)
        def _():
            add_half(0, expo.at[s], 0, weight, features, squared)

        @pl.when(s == CHUNKS - 2)
        def _():
            push(moments.at[0], sibling, send_one.at[11], recv_one.at[11], dst=got_moments)
            push(mass.at[0], sibling, send_one.at[12], recv_one.at[12], dst=got_mass)

        @pl.when(s == CHUNKS - 1)
        def _():
            scales[...] = jnp.broadcast_to(weight, (8, 512))
            push(scales, sibling, send_one.at[16], recv_one.at[16], dst=far_scale)

        add_half(1, expo.at[s], 256, weight, features, squared)

    @pl.loop(0, CHUNKS + LAG_M)
    def _(it):
        @pl.when(it < CHUNKS)
        def _():
            s = it
            i, j = s // 4, s % 4
            arrived(grid.at[0, 0, 0], recv_hop.at[s])
            @pl.when(s + AHEAD < CHUNKS)
            def _():
                hop(s + AHEAD)

            step = 1 - 2 * (s % 2)
            for axis, ref in third(i, j, 4 - step):
                push(ref, along(axis, 4 + step), send_fwd.at[s], recv_fwd.at[s])

        @pl.when((it >= LAG_A) & (it < CHUNKS + LAG_A))
        def _():
            s = it - LAG_A
            arrived(stat_a.at[s, pl.ds(0, 7)], recv_a.at[s])
            top, total = combine(stat_a.at[s])
            stat_b[s, slot_b] = jnp.concatenate([top, total], axis=0)
            for k in range(1, 8):
                push(stat_b.at[s, slot_b], peer_b(k), send_b.at[s], recv_b.at[s])

        @pl.when((it >= LAG_L) & (it < CHUNKS + LAG_L))
        def _():
            s = it - LAG_L
            arrived(grid.at[0, 0, 0, pl.ds(0, 2)], recv_fwd.at[s])
            logits_of(s)
            for k in range(1, 8):
                push(stat_a.at[s, slot_a], peer_a(k), send_a.at[s], recv_a.at[s])

            @pl.when(s == CHUNKS - 1)
            def _():
                push(grid.at[1, 3, 0], sibling, send_one.at[14], recv_one.at[14], dst=far_rows.at[pl.ds(0, 4)])
                push(grid.at[1, 3, 1], sibling, send_one.at[14], recv_one.at[14], dst=far_rows.at[pl.ds(4, 4)])
                push(expo.at[s, pl.ds(0, 256)], sibling, send_one.at[15], recv_one.at[15], dst=far_expo)

        @pl.when(it >= LAG_M)
        def _():
            s = it - LAG_M
            arrived(stat_b.at[s, pl.ds(0, 7)], recv_b.at[s])
            top, total = combine(stat_b.at[s])
            log_total = top + jnp.log(total)
            mask = masks[s][0:1, :]
            scale = jnp.exp(peaks[s][0:4] - log_total)
            scale = jnp.concatenate([scale[k:k + 1, :] for k in range(4)], axis=1) * mask
            score = jnp.concatenate([log_total[k:k + 1, :] for k in range(4)], axis=1) * mask
            score_acc[0:1, :] += score
            moments_of(s, scale)

    score_plane = jnp.sum(score_acc[0:1, :], axis=1, keepdims=True)
    score_mine[...] = jnp.concatenate([jnp.broadcast_to(score_plane, (4, LANES)), jnp.broadcast_to(count_plane, (4, LANES))], axis=0)
    push(score_mine, sibling, send_one.at[13], recv_one.at[13], dst=score_got)
    arrived(far_rows, recv_one.at[14])
    arrived(far_expo, recv_one.at[15])
    arrived(far_scale, recv_one.at[16])

    def far_squared(n, xs):
        wide = xs.astype(F32)
        return (wide * wide).astype(BF16)

    add_half(1, far_expo, 0, far_scale[0:1, :], lambda f: far_rows[f], far_squared)

    arrived(score_got, recv_one.at[13])
    arrived(got_mass, recv_one.at[12])
    arrived(got_moments, recv_one.at[11])

    sent(give, send_one.at[0])
    sent(far_rows, send_one.at[14])
    sent(far_expo, send_one.at[15])
    sent(scales, send_one.at[16])
    for part_no in range(3):
        sent(first_done[part_no], send_one.at[1 + part_no])
        sent(second_done[part_no], send_one.at[4 + part_no])
    sent(weights.at[1], send_one.at[7])
    sent(offsets.at[1], send_one.at[8])
    sent(valids.at[0, pl.ds(0, 3)], send_one.at[9])
    sent(valids.at[0], send_one.at[10])
    sent(moments.at[0], send_one.at[11])
    sent(mass.at[0], send_one.at[12])
    sent(score_mine, send_one.at[13])

    @pl.loop(0, CHUNKS)
    def _(s):
        sent(grid.at[0, 0, 0], send_hop.at[s])
        sent(grid.at[0, 0, 0, pl.ds(0, 2)], send_fwd.at[s])
        sent(stat_a.at[s, pl.ds(0, 7)], send_a.at[s])
        sent(stat_b.at[s, pl.ds(0, 7)], send_b.at[s])


def finish(moments, got_moments, mass, got_mass, means, prec, score_mine, score_got,
           out_means, out_vars, out_weights, out_score, stage_means, stage_vars, means_sem, vars_sem):
    both = score_mine[...] + score_got[...]
    count = jnp.maximum(both[4:5, 0:1], 1.0)
    out_score[...] = both[0:1, :] / count
    copies = []
    for block in range(4):
        weights = []
        for tile in range(2):
            rows = pl.ds(block * 64 + tile * 32, 32)
            weight = jnp.sum(mass[1, rows, :] + got_mass[rows, :], axis=1, keepdims=True)
            weights.append(jnp.broadcast_to(weight, (32, LANES)))
            scale = 1.0 / (weight + PRIOR_MASS)
            c = means[rows, :].astype(F32)
            p = prec[rows, :].astype(F32)
            m = (moments[1, rows, 0:1024] + got_moments[rows, 0:1024] + PRIOR_MASS * c) * scale
            stage_means[rows, :] = m
            second = moments[1, rows, 1024:2048] + got_moments[rows, 1024:2048]
            stage_vars[rows, :] = (second + PRIOR_MASS * (1.0 / p + c * c)) * scale - m * m
        rows = pl.ds(block * 64, 64)
        copies.append(pltpu.make_async_copy(stage_means.at[rows], out_means.at[rows], means_sem.at[block]))
        copies.append(pltpu.make_async_copy(stage_vars.at[rows], out_vars.at[rows], vars_sem.at[block]))
        copies[-2].start()
        copies[-1].start()
        weights = jnp.concatenate(weights + weights, axis=0)
        out_weights[block // 2:block // 2 + 1, (block % 2) * 64:(block % 2) * 64 + 64] = jnp.transpose(weights)[0:1, 0:64] / count
    for copy in copies:
        copy.wait()


def functools_sum(items):
    total = items[0]
    for item in items[1:]:
        total = total + item
    return total


def per_device(embeddings, means, precisions, log_weights, valid):
    hbm = pl.BlockSpec(memory_space=pltpu.HBM)
    vmem = pl.BlockSpec(memory_space=pltpu.VMEM)
    dma = pltpu.SemaphoreType.DMA
    found = pl.pallas_call(
        kernel,
        out_shape=(
            pltpu.VMEM((2, 256, 2048), F32),
            pltpu.VMEM((256, 2048), F32),
            pltpu.VMEM((2, 256, LANES), F32),
            pltpu.VMEM((256, LANES), F32),
            pltpu.VMEM((256, 1024), BF16),
            pltpu.VMEM((256, 1024), BF16),
            pltpu.VMEM((8, LANES), F32),
            pltpu.VMEM((8, LANES), F32),
        ),
        in_specs=[hbm] * 5,
        out_specs=[vmem] * 8,
        scratch_shapes=[
            pltpu.VMEM((64, 512), BF16),
            pltpu.VMEM((16, LANES), F32),
            pltpu.VMEM((8, LANES), jnp.int32),
            pltpu.VMEM((64, 512), BF16),
            pltpu.VMEM((2, 4, 2, 4, 512, LANES), BF16),
            pltpu.VMEM((2, 256, 2048), BF16),
            pltpu.VMEM((2, 256, LANES), F32),
            pltpu.VMEM((2, 4, 8, LANES), F32),
            pltpu.VMEM((CHUNKS, 8, 512), F32),
            pltpu.VMEM((CHUNKS, 512, 1024), BF16),
            pltpu.VMEM((CHUNKS, 512, 512), F32),
            pltpu.VMEM((CHUNKS, 8, LANES), F32),
            pltpu.VMEM((CHUNKS, 8, 8, LANES), F32),
            pltpu.VMEM((CHUNKS, 8, 8, LANES), F32),
            pltpu.VMEM((256, 512), BF16),
            pltpu.VMEM((8, 512, LANES), BF16),
            pltpu.VMEM((256, 512), F32),
            pltpu.VMEM((8, 512), F32),
            pltpu.VMEM((8, 512), F32),
            pltpu.VMEM((8, 512), F32),
            dma((5,)),
            dma((17,)), dma((17,)),
            dma((CHUNKS,)), dma((CHUNKS,)),
            dma((CHUNKS,)), dma((CHUNKS,)),
            dma((CHUNKS,)), dma((CHUNKS,)),
            dma((CHUNKS,)), dma((CHUNKS,)),
        ],
        compiler_params=pltpu.CompilerParams(
            collective_id=0, has_side_effects=True, vmem_limit_bytes=48 << 20
        ),
        cost_estimate=pl.CostEstimate(flops=17 << 30, bytes_accessed=8 << 20, transcendentals=4 << 20),
        name="mixture_step",
    )(embeddings.T, means, precisions, log_weights.reshape(16, LANES), valid.reshape(8, LANES))
    new_means, new_vars, weights, score = pl.pallas_call(
        finish,
        out_shape=(
            jax.ShapeDtypeStruct((256, 1024), F32),
            jax.ShapeDtypeStruct((256, 1024), F32),
            jax.ShapeDtypeStruct((2, LANES), F32),
            jax.ShapeDtypeStruct((1, LANES), F32),
        ),
        in_specs=[vmem] * 8,
        out_specs=[hbm, hbm, vmem, vmem],
        scratch_shapes=[pltpu.VMEM((256, 1024), F32), pltpu.VMEM((256, 1024), F32), dma((4,)), dma((4,))],
        cost_estimate=pl.CostEstimate(flops=4 << 20, bytes_accessed=2 << 20, transcendentals=0),
        name="new_parameters",
    )(*found)
    return new_means, new_vars, weights.reshape(256), score[0, 0]


def solution(mesh):
    in_specs = (P("dp", "comp"), P("comp", None), P("comp", None), P("comp"), P("dp"))
    out_specs = (P(("comp", "dp"), None), P(("comp", "dp"), None), P(("comp", "dp")), P())
    return jax.shard_map(
        per_device, mesh=mesh, in_specs=in_specs, out_specs=out_specs, check_vma=False
    )
```

```python
import math

import jax
import jax.numpy as jnp
from jax import lax
from jax.sharding import PartitionSpec as P
import jax.experimental.pallas as pl
import jax.experimental.pallas.tpu as pltpu

PRIOR_MASS = 1.0
MESH = pl.DeviceIdType.MESH
F32, BF16 = jnp.float32, jnp.bfloat16

SIZE = ((32, 96, 96), (48, 80, 80))
BASE = ((0, 128, 320), (0, 192, 352))
FROM_0, FROM_1, FROM_2 = (0, 32, 80, 112), (160, 256), (336, 432)
CHUNKS = 8
AHEAD = 2
LAG_L, LAG_A, LAG_M = 2, 4, 6
LANES = 128
CONTRACT_LAST = (((1,), (1,)), ((), ()))
CONTRACT = (((1,), (0,)), ((), ()))


def kernel(emb_hbm, means_hbm, prec_hbm, lw_hbm, valid_hbm,
           out_means, out_vars, out_weights, out_score,
           moments, got_moments, mass, got_mass, means, prec, score_mine, score_got,
           emb, lw_ref, valid_ref, take, grid, weights, offsets, valids, masks,
           squares, expo, peaks, stat_a, stat_b, resp, far_rows, far_expo, scales, far_scale, score_acc,
           load_sem, send_one, recv_one, send_two, recv_two, send_x, recv_x, send_far, recv_far, send_hop, recv_hop, send_fwd, recv_fwd, send_a, recv_a, send_b, recv_b):
    dp, comp = lax.axis_index("dp"), lax.axis_index("comp")
    xh, y = dp // 4, dp % 4
    xl, z, core = comp // 8, (comp // 2) % 4, comp % 2
    x = xh * 2 + xl
    temper = 0.5 * math.sqrt(1024)

    def dev(x, y, z, core):
        return ((x // 2) * 4 + y, (x % 2) * 8 + z * 2 + core)

    def along(axis, step):
        if axis == "x":
            return dev((x + step) % 4, y, z, core)
        if axis == "y":
            return dev(x, (y + step) % 4, z, core)
        return dev(x, y, (z + step) % 4, core)

    sibling = dev(x, y, z, 1 - core)
    slot_a = x * 2 + y % 2
    slot_b = z * 2 + y // 2

    def peer_a(k):
        to = (slot_a + k) % 8
        return dev(to // 2, (y // 2) * 2 + to % 2, z, core)

    def peer_b(k):
        to = (slot_b + k) % 8
        return dev(x, (to % 2) * 2 + y % 2, to // 2, core)

    def push(ref, to, ssem, rsem, dst=None):
        pltpu.make_async_remote_copy(
            src_ref=ref, dst_ref=ref if dst is None else dst, send_sem=ssem, recv_sem=rsem, device_id=to, device_id_type=MESH
        ).start()

    def arrived(ref, rsem):
        pltpu.make_async_remote_copy(
            src_ref=ref, dst_ref=ref, send_sem=send_one.at[0], recv_sem=rsem, device_id=sibling, device_id_type=MESH
        ).wait_recv()

    def sent(ref, ssem):
        pltpu.make_async_remote_copy(
            src_ref=ref, dst_ref=ref, send_sem=ssem, recv_sem=recv_one.at[0], device_id=sibling, device_id_type=MESH
        ).wait_send()

    own = pl.multiple_of(dp * 256, 256)
    load_emb = pltpu.make_async_copy(emb_hbm.at[:, pl.ds(pl.multiple_of(core * 512, 512), 512)], emb, load_sem.at[0])
    load_means = pltpu.make_async_copy(means_hbm.at[pl.ds(own, 256)], means, load_sem.at[1])
    load_prec = pltpu.make_async_copy(prec_hbm.at[pl.ds(own, 256)], prec, load_sem.at[2])
    load_lw = pltpu.make_async_copy(lw_hbm, lw_ref, load_sem.at[3])
    load_valid = pltpu.make_async_copy(valid_hbm, valid_ref, load_sem.at[4])
    load_emb.start()
    load_valid.start()
    load_lw.start()
    load_means.start()
    load_prec.start()

    barrier = pltpu.get_barrier_semaphore()
    friends = [sibling]
    for k in range(1, 4):
        friends += [along("x", k), along("y", k), along("z", k)]
        friends += []
    for k in range(4):
        if k:
            friends.append(dev((x + k) % 4, (y // 2) * 2 + 1 - y % 2, z, core))
            friends.append(dev(x, (y + 2) % 4, (z + k) % 4, core))
    for friend in friends:
        pl.semaphore_signal(barrier, inc=1, device_id=friend, device_id_type=MESH)
    pl.semaphore_wait(barrier, len(friends))

    give = emb_hbm.at[:, pl.ds(pl.multiple_of((1 - core) * 512, 512), 512)]
    push(give, sibling, send_one.at[0], recv_one.at[0], dst=take)
    load_valid.wait()
    vrow = jnp.where(core == 0, valid_ref[0:4, :], valid_ref[4:8, :]).astype(F32)
    valids[xh, y] = jnp.concatenate([vrow, vrow], axis=0)
    for k in range(1, 4):
        push(valids.at[xh, y], along("y", k), send_one.at[9], recv_one.at[9])
    load_emb.wait()
    arrived(take, recv_one.at[0])
    kept, taken = emb[...], take[...]
    shard = jnp.concatenate([jnp.where(core == 0, kept, taken), jnp.where(core == 0, taken, kept)], axis=0)
    shard = jnp.transpose(shard)
    def rows_of(part, par, index):
        n = SIZE[par][part]
        return pl.ds(pl.multiple_of(BASE[par][part] + index * n, 16), n)

    for par in range(2):
        for jh in range(2):
            at = FROM_0[2 * jh + par]
            grid[xh, jh, par, xl, z, rows_of(0, par, y), :] = shard[at:at + SIZE[par][0]]
        at = FROM_1[par]
        grid[xh, y // 2, par, xl, z, rows_of(1, par, y % 2), :] = shard[at:at + SIZE[par][1]]
        at = FROM_2[par]
        grid[y // 2, y % 2, par, xl, z, rows_of(2, par, xh), :] = shard[at:at + SIZE[par][2]]

    first = []
    for par in range(2):
        first += [
            (0, "z", grid.at[xh, :, par, xl, z, rows_of(0, par, y)]),
            (1, "x", grid.at[xh, y // 2, par, xl, z, rows_of(1, par, y % 2)]),
            (2, "y", grid.at[y // 2, y % 2, par, xl, z, rows_of(2, par, xh)]),
        ]
    for k in range(1, 4):
        for part_no, axis, ref in first:
            push(ref, along(axis, k), send_one.at[1 + part_no], recv_one.at[1 + part_no])

    load_means.wait()
    load_prec.wait()
    load_lw.wait()
    for tile in range(2):
        row = jnp.broadcast_to(lw_ref[pl.ds(dp * 2 + tile, 1), :], (LANES, LANES))
        offsets[1, tile * LANES:(tile + 1) * LANES, :] = jnp.transpose(row)

    @pl.loop(0, 8)
    def _(t):
        rows = pl.ds(pl.multiple_of(t * 32, 32), 32)
        p = prec[rows, :].astype(F32)
        c = means[rows, :].astype(F32)
        scaled = (p * c).astype(BF16).astype(F32)
        halfp = (0.5 * p).astype(BF16).astype(F32)
        weights[1, rows, 0:1024] = (scaled * (1.0 / temper)).astype(BF16)
        weights[1, rows, 1024:2048] = (halfp * (-1.0 / temper)).astype(BF16)
        both = 0.5 * jnp.sum(jnp.log(p), axis=1, keepdims=True) - 0.5 * jnp.sum(p * c * c, axis=1, keepdims=True)
        offsets[1, rows, :] = (offsets[1, rows, :] + both) * (1.0 / temper)

    push(weights.at[1], sibling, send_one.at[7], recv_one.at[7], dst=weights.at[0])
    push(offsets.at[1], sibling, send_one.at[8], recv_one.at[8], dst=offsets.at[0])

    def blocks(n, rows):
        return grid.at[0, 0, 0, pl.ds(0, n // 4), :, pl.ds(0, rows)] if n % 4 == 0 else grid.at[0, 0, 0, 0, pl.ds(0, n), pl.ds(0, rows)]

    first_done = (blocks(3, 160), blocks(3, 176), blocks(3, 176))
    second_one = blocks(4, 160)
    second_done = blocks(3, 352)

    def second(part_no, group):
        for par in range(2):
            if part_no == 1:
                axis, ref = "y", grid.at[group, y // 2, par, :, z, rows_of(1, par, y % 2)]
            else:
                axis, ref = "z", grid.at[group, :, par, xl, z, rows_of(2, par, xh)]
            for k in range(1, 4):
                push(ref, along(axis, k), send_two.at[part_no, group], recv_two.at[part_no, group])

    def second_rows():
        for par in range(2):
            for k in range(1, 4):
                push(grid.at[xh, :, par, xl, :, rows_of(0, par, y)], along("x", k), send_x.at[k], recv_x.at[k])

    def second_here(group):
        for k in range(1, 4):
            @pl.when(((x + 4 - k) % 4) // 2 == group)
            def _():
                arrived(second_one, recv_x.at[k])

        arrived(second_done, recv_two.at[1, group])
        arrived(second_done, recv_two.at[2, group])

    arrived(first_done[0], recv_one.at[1])
    second_rows()
    for part_no in (1, 2):
        arrived(first_done[part_no], recv_one.at[1 + part_no])
        second(part_no, 0)
    for part_no in (1, 2):
        second(part_no, 1)
    arrived(valids.at[0, pl.ds(0, 3)], recv_one.at[9])
    push(valids.at[xh], along("x", 2), send_one.at[10], recv_one.at[10])

    moments[...] = jnp.zeros_like(moments)
    mass[...] = jnp.zeros_like(mass)
    score_acc[...] = jnp.zeros_like(score_acc)

    def third(s, par, step):
        i, jh = s // 4, (s // 2) % 2
        yy, zz, xx = (y + step) % 4, (z + step) % 4, (x + step) % 4
        return (
            ("y", grid.at[i, jh, par, :, :, rows_of(0, par, yy)]),
            ("z", grid.at[i, jh, par, :, zz, pl.ds(BASE[par][1], 2 * SIZE[par][1])]),
            ("x", grid.at[i, jh, par, xx % 2, :, rows_of(2, par, xx // 2)]),
        )

    def hop(s, par):
        for axis, ref in third(s, par, 0):
            for step in (1, 3):
                push(ref, along(axis, step), send_hop.at[s], recv_hop.at[s])

    def forward(s, par):
        i, jh = s // 4, (s // 2) % 2
        for half, step in ((0, 1), (1, 3)):
            yy, zz, xx = (y + 4 - step) % 4, (z + 4 - step) % 4, (x + 4 - step) % 4
            for axis, ref in (
                ("y", grid.at[i, jh, par, half, :, rows_of(0, par, yy)]),
                ("z", grid.at[i, jh, par, half, zz, pl.ds(BASE[par][1], 2 * SIZE[par][1])]),
                ("x", grid.at[i, jh, par, xx % 2, pl.ds(2 * half, 2), rows_of(2, par, xx // 2)]),
            ):
                push(ref, along(axis, step), send_fwd.at[s], recv_fwd.at[s])

    second_here(0)
    for s in range(AHEAD):
        hop(s, s % 2)

    arrived(valids.at[0], recv_one.at[10])
    place = lax.broadcasted_iota(jnp.int32, (8, 512), 1)

    def lanes_of(block):
        v = valids[block // 4, block % 4]
        return jnp.broadcast_to(jnp.concatenate([v[i:i + 1, :] for i in range(4)], axis=1), (8, 512))

    by_block = [lanes_of(b) for b in range(8)]
    count_plane = functools_sum([jnp.sum(b[0:1, :], axis=1, keepdims=True) for b in by_block])
    for s in range(CHUNKS):
        par = s % 2
        n0, n1, n2 = SIZE[par]
        b0, b1, b2 = BASE[par]
        out = by_block[s]
        for yy in range(4):
            moved = pltpu.roll(by_block[(s // 4) * 4 + yy], (yy * n0 - FROM_0[s % 4]) % 512, 1)
            out = jnp.where((place >= yy * n0) & (place < (yy + 1) * n0), moved, out)
        for k in range(2):
            at = b1 + k * n1
            moved = pltpu.roll(by_block[(s // 2) * 2 + k], (at - FROM_1[par]) % 512, 1)
            out = jnp.where((place >= at) & (place < at + n1), moved, out)
            at = b2 + k * n2
            moved = pltpu.roll(by_block[k * 4 + s // 2], (at - FROM_2[par]) % 512, 1)
            out = jnp.where((place >= at) & (place < at + n2), moved, out)
        masks[s] = out

    arrived(weights.at[0], recv_one.at[7])
    arrived(offsets.at[0], recv_one.at[8])

    def logits_of(s):
        chunk, slot = grid.at[s // 4, (s // 2) % 2, s % 2], s
        tops, sums = [], []
        for n in range(2):
            rows = pl.ds(n * 256, 256)
            xs = jnp.concatenate([chunk[f // 4, f % 4, rows, :] for f in range(8)], axis=1)
            wide = xs.astype(F32)
            sq = (wide * wide).astype(BF16)
            squares[slot, rows, :] = sq
            w = weights[...].reshape(512, 2048)
            l = lax.dot_general(w[:, 0:1024], xs, CONTRACT_LAST, preferred_element_type=F32)
            l = l + lax.dot_general(w[:, 1024:2048], sq, CONTRACT_LAST, preferred_element_type=F32)
            off = offsets[...].reshape(512, LANES)
            l = l + jnp.concatenate([off, off], axis=1)
            top = jnp.max(l, axis=0, keepdims=True)
            e = jnp.exp(l - top)
            expo[slot, :, rows] = e
            total = jnp.sum(e, axis=0, keepdims=True)
            tops += [top[:, 0:128], top[:, 128:256]]
            sums += [total[:, 0:128], total[:, 128:256]]
        stat = jnp.concatenate(tops + sums, axis=0)
        stat_a[s, slot_a] = stat
        peaks[slot] = stat

    def combine(ref):
        both = [ref[k] for k in range(8)]
        top = both[0][0:4]
        for b in both[1:]:
            top = jnp.maximum(top, b[0:4])
        total = jnp.zeros_like(top)
        for b in both:
            total = total + b[4:8] * jnp.exp(b[0:4] - top)
        return top, total

    def add_half(half, e_ref, row0, weight, features, squared):
        for part in range(2):
            r = (e_ref[pl.ds(row0 + part * 128, 128), :] * weight).astype(BF16)
            resp[pl.ds(part * 128, 128), :] = r
            wide = r.astype(F32)
            mass[half, pl.ds(part * 128, 128), :] += wide[:, 0:128] + wide[:, 128:256] + wide[:, 256:384] + wide[:, 384:512]
        r = resp[...]
        for n in range(4):
            xs = jnp.concatenate([features(2 * n), features(2 * n + 1)], axis=1)
            moments[half, :, n * 256:(n + 1) * 256] += lax.dot_general(r, xs, CONTRACT, preferred_element_type=F32)
            sq = squared(n, xs)
            moments[half, :, 1024 + n * 256:1024 + (n + 1) * 256] += lax.dot_general(r, sq, CONTRACT, preferred_element_type=F32)

    def moments_of(s, weight):
        chunk = grid.at[s // 4, (s // 2) % 2, s % 2]

        def features(f):
            return chunk[f // 4, f % 4]

        def squared(n, xs):
            return squares[s, :, n * 256:(n + 1) * 256]

        @pl.when(s < CHUNKS - 1)
        def _():
            add_half(0, expo.at[s], 0, weight, features, squared)

        @pl.when(s == CHUNKS - 2)
        def _():
            push(moments.at[0], sibling, send_one.at[11], recv_one.at[11], dst=got_moments)
            push(mass.at[0], sibling, send_one.at[12], recv_one.at[12], dst=got_mass)

        @pl.when(s == CHUNKS - 1)
        def _():
            scales[...] = jnp.broadcast_to(weight, (8, 512))
            push(scales, sibling, send_one.at[16], recv_one.at[16], dst=far_scale)

        add_half(1, expo.at[s], 256, weight, features, squared)

    @pl.loop(0, CHUNKS + LAG_M)
    def _(it):
        @pl.when(it < CHUNKS)
        def _():
            s = it

            @pl.when(s + AHEAD == 4)
            def _():
                second_here(1)

            arrived(blocks(4, 512), recv_hop.at[s])
            for par in range(2):
                @pl.when((s % 2 == par) & (s < CHUNKS - 1))
                def _():
                    forward(s, par)

                @pl.when(((s + AHEAD) % 2 == par) & (s + AHEAD < CHUNKS))
                def _():
                    hop(s + AHEAD, par)

            @pl.when(s + AHEAD == CHUNKS - 1)
            def _():
                for axis, ref in third(CHUNKS - 1, 1, 0):
                    push(ref, along(axis, 2), send_far.at[0], recv_far.at[0])

            @pl.when(s == CHUNKS - 1)
            def _():
                arrived(blocks(2, 512), recv_far.at[0])

        @pl.when((it >= LAG_A) & (it < CHUNKS + LAG_A))
        def _():
            s = it - LAG_A
            arrived(stat_a.at[s, pl.ds(0, 7)], recv_a.at[s])
            top, total = combine(stat_a.at[s])
            stat_b[s, slot_b] = jnp.concatenate([top, total], axis=0)
            for k in range(1, 8):
                push(stat_b.at[s, slot_b], peer_b(k), send_b.at[s], recv_b.at[s])

        @pl.when((it >= LAG_L) & (it < CHUNKS + LAG_L))
        def _():
            s = it - LAG_L
            @pl.when(s < CHUNKS - 1)
            def _():
                arrived(blocks(2, 512), recv_fwd.at[s])

            logits_of(s)
            for k in range(1, 8):
                push(stat_a.at[s, slot_a], peer_a(k), send_a.at[s], recv_a.at[s])

            @pl.when(s == CHUNKS - 1)
            def _():
                push(grid.at[1, 1, 1, 0], sibling, send_one.at[14], recv_one.at[14], dst=far_rows.at[pl.ds(0, 4)])
                push(grid.at[1, 1, 1, 1], sibling, send_one.at[14], recv_one.at[14], dst=far_rows.at[pl.ds(4, 4)])
                push(expo.at[s, pl.ds(0, 256)], sibling, send_one.at[15], recv_one.at[15], dst=far_expo)

        @pl.when(it >= LAG_M)
        def _():
            s = it - LAG_M
            arrived(stat_b.at[s, pl.ds(0, 7)], recv_b.at[s])
            top, total = combine(stat_b.at[s])
            log_total = top + jnp.log(total)
            mask = masks[s][0:1, :]
            scale = jnp.exp(peaks[s][0:4] - log_total)
            scale = jnp.concatenate([scale[k:k + 1, :] for k in range(4)], axis=1) * mask
            score = jnp.concatenate([log_total[k:k + 1, :] for k in range(4)], axis=1) * mask
            score_acc[0:1, :] += score
            moments_of(s, scale)

    score_plane = jnp.sum(score_acc[0:1, :], axis=1, keepdims=True)
    score_mine[...] = jnp.concatenate([jnp.broadcast_to(score_plane, (4, LANES)), jnp.broadcast_to(count_plane, (4, LANES))], axis=0)
    push(score_mine, sibling, send_one.at[13], recv_one.at[13], dst=score_got)
    arrived(far_rows, recv_one.at[14])
    arrived(far_expo, recv_one.at[15])
    arrived(far_scale, recv_one.at[16])

    def far_squared(n, xs):
        wide = xs.astype(F32)
        return (wide * wide).astype(BF16)

    add_half(1, far_expo, 0, far_scale[0:1, :], lambda f: far_rows[f], far_squared)

    arrived(score_got, recv_one.at[13])
    arrived(got_mass, recv_one.at[12])
    arrived(got_moments, recv_one.at[11])

    both = score_mine[...] + score_got[...]
    count = jnp.maximum(both[4:5, 0:1], 1.0)
    out_score[...] = both[0:1, :] / count

    @pl.loop(0, 8)
    def _(t):
        rows = pl.ds(pl.multiple_of(t * 32, 32), 32)
        weight = jnp.sum(mass[1, rows, :] + got_mass[rows, :], axis=1, keepdims=True)
        got_mass[rows, :] = jnp.broadcast_to(weight, (32, LANES))
        scale = 1.0 / (weight + PRIOR_MASS)
        c = means[rows, :].astype(F32)
        p = prec[rows, :].astype(F32)
        m = (moments[1, rows, 0:1024] + got_moments[rows, 0:1024] + PRIOR_MASS * c) * scale
        out_means[rows, :] = m
        out_vars[rows, :] = (moments[1, rows, 1024:2048] + got_moments[rows, 1024:2048] + PRIOR_MASS * (1.0 / p + c * c)) * scale - m * m

    for tile in range(2):
        out_weights[tile:tile + 1, :] = jnp.transpose(got_mass[tile * LANES:(tile + 1) * LANES, :])[0:1, :] / count

    sent(blocks(2, 512), send_far.at[0])
    sent(give, send_one.at[0])
    sent(far_rows, send_one.at[14])
    sent(far_expo, send_one.at[15])
    sent(scales, send_one.at[16])
    for part_no in range(3):
        sent(first_done[part_no], send_one.at[1 + part_no])
    for k in range(1, 4):
        sent(second_one, send_x.at[k])
    for group in range(2):
        sent(second_done, send_two.at[1, group])
        sent(second_done, send_two.at[2, group])
    sent(weights.at[1], send_one.at[7])
    sent(offsets.at[1], send_one.at[8])
    sent(valids.at[0, pl.ds(0, 3)], send_one.at[9])
    sent(valids.at[0], send_one.at[10])
    sent(moments.at[0], send_one.at[11])
    sent(mass.at[0], send_one.at[12])
    sent(score_mine, send_one.at[13])

    @pl.loop(0, CHUNKS)
    def _(s):
        sent(blocks(4, 512), send_hop.at[s])

        @pl.when(s < CHUNKS - 1)
        def _():
            sent(blocks(2, 512), send_fwd.at[s])

        sent(stat_a.at[s, pl.ds(0, 7)], send_a.at[s])
        sent(stat_b.at[s, pl.ds(0, 7)], send_b.at[s])


def functools_sum(items):
    total = items[0]
    for item in items[1:]:
        total = total + item
    return total


def per_device(embeddings, means, precisions, log_weights, valid):
    hbm = pl.BlockSpec(memory_space=pltpu.HBM)
    vmem = pl.BlockSpec(memory_space=pltpu.VMEM)
    dma = pltpu.SemaphoreType.DMA
    new_means, new_vars, weights, score = pl.pallas_call(
        kernel,
        out_shape=(
            pltpu.VMEM((256, 1024), F32),
            pltpu.VMEM((256, 1024), F32),
            pltpu.VMEM((2, LANES), F32),
            pltpu.VMEM((1, LANES), F32),
        ),
        in_specs=[hbm] * 5,
        out_specs=[vmem] * 4,
        scratch_shapes=[
            pltpu.VMEM((2, 256, 2048), F32),
            pltpu.VMEM((256, 2048), F32),
            pltpu.VMEM((2, 256, LANES), F32),
            pltpu.VMEM((256, LANES), F32),
            pltpu.VMEM((256, 1024), BF16),
            pltpu.VMEM((256, 1024), BF16),
            pltpu.VMEM((8, LANES), F32),
            pltpu.VMEM((8, LANES), F32),
            pltpu.VMEM((64, 512), BF16),
            pltpu.VMEM((16, LANES), F32),
            pltpu.VMEM((8, LANES), jnp.int32),
            pltpu.VMEM((64, 512), BF16),
            pltpu.VMEM((2, 2, 2, 2, 4, 512, LANES), BF16),
            pltpu.VMEM((2, 256, 2048), BF16),
            pltpu.VMEM((2, 256, LANES), F32),
            pltpu.VMEM((2, 4, 8, LANES), F32),
            pltpu.VMEM((CHUNKS, 8, 512), F32),
            pltpu.VMEM((CHUNKS, 512, 1024), BF16),
            pltpu.VMEM((CHUNKS, 512, 512), F32),
            pltpu.VMEM((CHUNKS, 8, LANES), F32),
            pltpu.VMEM((CHUNKS, 8, 8, LANES), F32),
            pltpu.VMEM((CHUNKS, 8, 8, LANES), F32),
            pltpu.VMEM((256, 512), BF16),
            pltpu.VMEM((8, 512, LANES), BF16),
            pltpu.VMEM((256, 512), F32),
            pltpu.VMEM((8, 512), F32),
            pltpu.VMEM((8, 512), F32),
            pltpu.VMEM((8, 512), F32),
            dma((5,)),
            dma((17,)), dma((17,)),
            dma((3, 2)), dma((3, 2)),
            dma((4,)), dma((4,)), dma((1,)), dma((1,)),
            dma((CHUNKS,)), dma((CHUNKS,)),
            dma((CHUNKS,)), dma((CHUNKS,)),
            dma((CHUNKS,)), dma((CHUNKS,)),
            dma((CHUNKS,)), dma((CHUNKS,)),
        ],
        compiler_params=pltpu.CompilerParams(
            collective_id=0, has_side_effects=True, vmem_limit_bytes=58 << 20
        ),
        cost_estimate=pl.CostEstimate(flops=17 << 30, bytes_accessed=8 << 20, transcendentals=4 << 20),
        name="mixture_step",
    )(embeddings.T, means, precisions, log_weights.reshape(16, LANES), valid.reshape(8, LANES))
    return new_means, new_vars, weights.reshape(256), score[0, 0]


def solution(mesh):
    in_specs = (P("dp", "comp"), P("comp", None), P("comp", None), P("comp"), P("dp"))
    out_specs = (P(("comp", "dp"), None), P(("comp", "dp"), None), P(("comp", "dp")), P())
    return jax.shard_map(
        per_device, mesh=mesh, in_specs=in_specs, out_specs=out_specs, check_vma=False
    )
```

```python
import math

import jax
import jax.numpy as jnp
from jax import lax
from jax.sharding import PartitionSpec as P
import jax.experimental.pallas as pl
import jax.experimental.pallas.tpu as pltpu

PRIOR_MASS = 1.0
MESH = pl.DeviceIdType.MESH
F32, BF16 = jnp.float32, jnp.bfloat16

SIZE = ((32, 96, 96), (48, 80, 80))
BASE = ((0, 128, 320), (0, 192, 352))
FROM_0, FROM_1, FROM_2 = (0, 32, 80, 112), (160, 256), (336, 432)
CHUNKS = 8
AHEAD = 3
SHARED = 2
ROUNDS = (0, 1, 4, 8)
LAG_L, LAG_A = 3, 7
LANES = 128
CONTRACT_LAST = (((1,), (1,)), ((), ()))
CONTRACT = (((1,), (0,)), ((), ()))


def kernel(emb_hbm, means_hbm, prec_hbm, lw_hbm, valid_hbm,
           moments, got_moments, mass, got_mass, means, prec, score_mine, score_got,
           emb, lw_ref, valid_ref, take, grid, weights, offsets, valids, masks,
           squares, expo, peaks, stat_a, stat_b, resp, far_rows, far_expo, scales, far_scale, score_acc,
           load_sem, send_one, recv_one, send_two, recv_two, send_x, recv_x, send_rows, recv_rows, send_expo, recv_expo, send_scale, recv_scale, send_far, recv_far, send_hop, recv_hop, send_fwd, recv_fwd, send_a, recv_a, send_b, recv_b):
    dp, comp = lax.axis_index("dp"), lax.axis_index("comp")
    xh, y = dp // 4, dp % 4
    xl, z, core = comp // 8, (comp // 2) % 4, comp % 2
    x = xh * 2 + xl
    temper = 0.5 * math.sqrt(1024)

    def dev(x, y, z, core):
        return ((x // 2) * 4 + y, (x % 2) * 8 + z * 2 + core)

    def along(axis, step):
        if axis == "x":
            return dev((x + step) % 4, y, z, core)
        if axis == "y":
            return dev(x, (y + step) % 4, z, core)
        return dev(x, y, (z + step) % 4, core)

    sibling = dev(x, y, z, 1 - core)
    slot_a = x * 2 + y % 2
    slot_b = z * 2 + y // 2

    def peer_a(k):
        to = (slot_a + k) % 8
        return dev(to // 2, (y // 2) * 2 + to % 2, z, core)

    def peer_b(k):
        to = (slot_b + k) % 8
        return dev(x, (to % 2) * 2 + y % 2, to // 2, core)

    def push(ref, to, ssem, rsem, dst=None):
        pltpu.make_async_remote_copy(
            src_ref=ref, dst_ref=ref if dst is None else dst, send_sem=ssem, recv_sem=rsem, device_id=to, device_id_type=MESH
        ).start()

    def arrived(ref, rsem):
        pltpu.make_async_remote_copy(
            src_ref=ref, dst_ref=ref, send_sem=send_one.at[0], recv_sem=rsem, device_id=sibling, device_id_type=MESH
        ).wait_recv()

    def sent(ref, ssem):
        pltpu.make_async_remote_copy(
            src_ref=ref, dst_ref=ref, send_sem=ssem, recv_sem=recv_one.at[0], device_id=sibling, device_id_type=MESH
        ).wait_send()

    own = pl.multiple_of(dp * 256, 256)
    load_emb = pltpu.make_async_copy(emb_hbm.at[:, pl.ds(pl.multiple_of(core * 512, 512), 512)], emb, load_sem.at[0])
    load_means = pltpu.make_async_copy(means_hbm.at[pl.ds(own, 256)], means, load_sem.at[1])
    load_prec = pltpu.make_async_copy(prec_hbm.at[pl.ds(own, 256)], prec, load_sem.at[2])
    load_lw = pltpu.make_async_copy(lw_hbm, lw_ref, load_sem.at[3])
    load_valid = pltpu.make_async_copy(valid_hbm, valid_ref, load_sem.at[4])
    load_emb.start()
    load_valid.start()
    load_lw.start()
    load_means.start()
    load_prec.start()

    barrier = pltpu.get_barrier_semaphore()
    friends = [sibling]
    for k in range(1, 4):
        friends += [along("x", k), along("y", k), along("z", k)]
        friends += []
    for k in range(4):
        if k:
            friends.append(dev((x + k) % 4, (y // 2) * 2 + 1 - y % 2, z, core))
            friends.append(dev(x, (y + 2) % 4, (z + k) % 4, core))
    for friend in friends:
        pl.semaphore_signal(barrier, inc=1, device_id=friend, device_id_type=MESH)
    pl.semaphore_wait(barrier, len(friends))

    give = emb_hbm.at[:, pl.ds(pl.multiple_of((1 - core) * 512, 512), 512)]
    push(give, sibling, send_one.at[0], recv_one.at[0], dst=take)
    load_valid.wait()
    vrow = jnp.where(core == 0, valid_ref[0:4, :], valid_ref[4:8, :]).astype(F32)
    valids[xh, y] = jnp.concatenate([vrow, vrow], axis=0)
    for k in range(1, 4):
        push(valids.at[xh, y], along("y", k), send_one.at[9], recv_one.at[9])
    load_emb.wait()
    arrived(take, recv_one.at[0])
    kept, taken = emb[...], take[...]
    shard = jnp.concatenate([jnp.where(core == 0, kept, taken), jnp.where(core == 0, taken, kept)], axis=0)
    shard = jnp.transpose(shard)
    def rows_of(part, par, index):
        n = SIZE[par][part]
        return pl.ds(pl.multiple_of(BASE[par][part] + index * n, 16), n)

    for par in range(2):
        for jh in range(2):
            at = FROM_0[2 * jh + par]
            grid[xh, jh, par, xl, z, rows_of(0, par, y), :] = shard[at:at + SIZE[par][0]]
        at = FROM_1[par]
        grid[xh, y // 2, par, xl, z, rows_of(1, par, y % 2), :] = shard[at:at + SIZE[par][1]]
        at = FROM_2[par]
        grid[y // 2, y % 2, par, xl, z, rows_of(2, par, xh), :] = shard[at:at + SIZE[par][2]]

    first = []
    for par in range(2):
        first += [
            (0, "z", grid.at[xh, :, par, xl, z, rows_of(0, par, y)]),
            (1, "x", grid.at[xh, y // 2, par, xl, z, rows_of(1, par, y % 2)]),
            (2, "y", grid.at[y // 2, y % 2, par, xl, z, rows_of(2, par, xh)]),
        ]
    for k in range(1, 4):
        for part_no, axis, ref in first:
            push(ref, along(axis, k), send_one.at[1 + part_no], recv_one.at[1 + part_no])

    load_means.wait()
    load_prec.wait()
    load_lw.wait()
    for tile in range(2):
        row = jnp.broadcast_to(lw_ref[pl.ds(dp * 2 + tile, 1), :], (LANES, LANES))
        offsets[1, tile * LANES:(tile + 1) * LANES, :] = jnp.transpose(row)

    @pl.loop(0, 8)
    def _(t):
        rows = pl.ds(pl.multiple_of(t * 32, 32), 32)
        p = prec[rows, :].astype(F32)
        c = means[rows, :].astype(F32)
        scaled = (p * c).astype(BF16).astype(F32)
        halfp = (0.5 * p).astype(BF16).astype(F32)
        weights[1, rows, 0:1024] = (scaled * (1.0 / temper)).astype(BF16)
        weights[1, rows, 1024:2048] = (halfp * (-1.0 / temper)).astype(BF16)
        both = 0.5 * jnp.sum(jnp.log(p), axis=1, keepdims=True) - 0.5 * jnp.sum(p * c * c, axis=1, keepdims=True)
        offsets[1, rows, :] = (offsets[1, rows, :] + both) * (1.0 / temper)

    push(weights.at[1], sibling, send_one.at[7], recv_one.at[7], dst=weights.at[0])
    push(offsets.at[1], sibling, send_one.at[8], recv_one.at[8], dst=offsets.at[0])

    def blocks(n, rows):
        return grid.at[0, 0, 0, pl.ds(0, n // 4), :, pl.ds(0, rows)] if n % 4 == 0 else grid.at[0, 0, 0, 0, pl.ds(0, n), pl.ds(0, rows)]

    first_done = (blocks(3, 160), blocks(3, 176), blocks(3, 176))
    second_one = blocks(4, 160)
    second_done = blocks(3, 352)

    def second(part_no, group):
        for par in range(2):
            if part_no == 1:
                axis, ref = "y", grid.at[group, y // 2, par, :, z, rows_of(1, par, y % 2)]
            else:
                axis, ref = "z", grid.at[group, :, par, xl, z, rows_of(2, par, xh)]
            for k in range(1, 4):
                push(ref, along(axis, k), send_two.at[part_no, group], recv_two.at[part_no, group])

    def second_rows():
        for par in range(2):
            for k in range(1, 4):
                push(grid.at[xh, :, par, xl, :, rows_of(0, par, y)], along("x", k), send_x.at[k], recv_x.at[k])

    def second_here(group):
        for k in range(1, 4):
            @pl.when(((x + 4 - k) % 4) // 2 == group)
            def _():
                arrived(second_one, recv_x.at[k])

        arrived(second_done, recv_two.at[1, group])
        arrived(second_done, recv_two.at[2, group])

    arrived(first_done[0], recv_one.at[1])
    second_rows()
    for part_no in (1, 2):
        arrived(first_done[part_no], recv_one.at[1 + part_no])
        second(part_no, 0)
    for part_no in (1, 2):
        second(part_no, 1)
    arrived(valids.at[0, pl.ds(0, 3)], recv_one.at[9])
    push(valids.at[xh], along("x", 2), send_one.at[10], recv_one.at[10])

    moments[...] = jnp.zeros_like(moments)
    mass[...] = jnp.zeros_like(mass)
    score_acc[...] = jnp.zeros_like(score_acc)

    def third(s, par, step):
        i, jh = s // 4, (s // 2) % 2
        yy, zz, xx = (y + step) % 4, (z + step) % 4, (x + step) % 4
        return (
            ("y", grid.at[i, jh, par, :, :, rows_of(0, par, yy)]),
            ("z", grid.at[i, jh, par, :, zz, pl.ds(BASE[par][1], 2 * SIZE[par][1])]),
            ("x", grid.at[i, jh, par, xx % 2, :, rows_of(2, par, xx // 2)]),
        )

    def hop(s, par):
        for axis, ref in third(s, par, 0):
            for step in (1, 3):
                push(ref, along(axis, step), send_hop.at[s], recv_hop.at[s])

    def forward(s, par):
        i, jh = s // 4, (s // 2) % 2
        for half, step in ((0, 1), (1, 3)):
            yy, zz, xx = (y + 4 - step) % 4, (z + 4 - step) % 4, (x + 4 - step) % 4
            for axis, ref in (
                ("y", grid.at[i, jh, par, half, :, rows_of(0, par, yy)]),
                ("z", grid.at[i, jh, par, half, zz, pl.ds(BASE[par][1], 2 * SIZE[par][1])]),
                ("x", grid.at[i, jh, par, xx % 2, pl.ds(2 * half, 2), rows_of(2, par, xx // 2)]),
            ):
                push(ref, along(axis, step), send_fwd.at[s], recv_fwd.at[s])

    second_here(0)
    for s in range(AHEAD):
        hop(s, s % 2)

    arrived(valids.at[0], recv_one.at[10])
    place = lax.broadcasted_iota(jnp.int32, (8, 512), 1)

    def lanes_of(block):
        v = valids[block // 4, block % 4]
        return jnp.broadcast_to(jnp.concatenate([v[i:i + 1, :] for i in range(4)], axis=1), (8, 512))

    by_block = [lanes_of(b) for b in range(8)]
    count_plane = functools_sum([jnp.sum(b[0:1, :], axis=1, keepdims=True) for b in by_block])
    for s in range(CHUNKS):
        par = s % 2
        n0, n1, n2 = SIZE[par]
        b0, b1, b2 = BASE[par]
        out = by_block[s]
        for yy in range(4):
            moved = pltpu.roll(by_block[(s // 4) * 4 + yy], (yy * n0 - FROM_0[s % 4]) % 512, 1)
            out = jnp.where((place >= yy * n0) & (place < (yy + 1) * n0), moved, out)
        for k in range(2):
            at = b1 + k * n1
            moved = pltpu.roll(by_block[(s // 2) * 2 + k], (at - FROM_1[par]) % 512, 1)
            out = jnp.where((place >= at) & (place < at + n1), moved, out)
            at = b2 + k * n2
            moved = pltpu.roll(by_block[k * 4 + s // 2], (at - FROM_2[par]) % 512, 1)
            out = jnp.where((place >= at) & (place < at + n2), moved, out)
        masks[s] = out

    arrived(weights.at[0], recv_one.at[7])
    arrived(offsets.at[0], recv_one.at[8])

    def logits_of(s):
        chunk, slot = grid.at[s // 4, (s // 2) % 2, s % 2], s
        tops, sums = [], []
        for n in range(2):
            rows = pl.ds(n * 256, 256)
            xs = jnp.concatenate([chunk[f // 4, f % 4, rows, :] for f in range(8)], axis=1)
            wide = xs.astype(F32)
            sq = (wide * wide).astype(BF16)
            squares[slot, rows, :] = sq
            w = weights[...].reshape(512, 2048)
            l = lax.dot_general(w[:, 0:1024], xs, CONTRACT_LAST, preferred_element_type=F32)
            l = l + lax.dot_general(w[:, 1024:2048], sq, CONTRACT_LAST, preferred_element_type=F32)
            off = offsets[...].reshape(512, LANES)
            l = l + jnp.concatenate([off, off], axis=1)
            top = jnp.max(l, axis=0, keepdims=True)
            e = jnp.exp(l - top)
            expo[slot, :, rows] = e
            total = jnp.sum(e, axis=0, keepdims=True)
            tops += [top[:, 0:128], top[:, 128:256]]
            sums += [total[:, 0:128], total[:, 128:256]]
        stat = jnp.concatenate(tops + sums, axis=0)
        stat_a[s, slot_a] = stat
        peaks[slot] = stat

    def combine(ref):
        both = [ref[k] for k in range(8)]
        top = both[0][0:4]
        for b in both[1:]:
            top = jnp.maximum(top, b[0:4])
        total = jnp.zeros_like(top)
        for b in both:
            total = total + b[4:8] * jnp.exp(b[0:4] - top)
        return top, total

    def add_half(half, e_ref, row0, weight, features, squared):
        for part in range(2):
            r = (e_ref[pl.ds(row0 + part * 128, 128), :] * weight).astype(BF16)
            resp[pl.ds(part * 128, 128), :] = r
            wide = r.astype(F32)
            mass[half, pl.ds(part * 128, 128), :] += wide[:, 0:128] + wide[:, 128:256] + wide[:, 256:384] + wide[:, 384:512]
        r = resp[...]
        for n in range(4):
            xs = jnp.concatenate([features(2 * n), features(2 * n + 1)], axis=1)
            moments[half, :, n * 256:(n + 1) * 256] += lax.dot_general(r, xs, CONTRACT, preferred_element_type=F32)
            sq = squared(n, xs)
            moments[half, :, 1024 + n * 256:1024 + (n + 1) * 256] += lax.dot_general(r, sq, CONTRACT, preferred_element_type=F32)

    def second_round(s):
        arrived(stat_a.at[s, pl.ds(0, 7)], recv_a.at[s])
        top, total = combine(stat_a.at[s])
        stat_b[s, slot_b] = jnp.concatenate([top, total], axis=0)
        for k in range(1, 8):
            push(stat_b.at[s, slot_b], peer_b(k), send_b.at[s], recv_b.at[s])

    def weigh(s):
        arrived(stat_b.at[s, pl.ds(0, 7)], recv_b.at[s])
        top, total = combine(stat_b.at[s])
        log_total = top + jnp.log(total)
        mask = masks[s][0:1, :]
        scale = jnp.exp(peaks[s][0:4] - log_total)
        scale = jnp.concatenate([scale[k:k + 1, :] for k in range(4)], axis=1) * mask
        score = jnp.concatenate([log_total[k:k + 1, :] for k in range(4)], axis=1) * mask
        score_acc[0:1, :] += score
        scales[s] = jnp.broadcast_to(scale, (8, 512))

    def add_chunk(half, s):
        chunk = grid.at[s // 4, (s // 2) % 2, s % 2]
        start = half * 256 if isinstance(half, int) else pl.multiple_of(half * 256, 256)
        add_half(half, expo.at[s], start, scales[s][0:1, :], lambda f: chunk[f // 4, f % 4],
                 lambda n, xs: squares[s, :, n * 256:(n + 1) * 256])

    @pl.loop(0, CHUNKS + LAG_L)
    def _(it):
        @pl.when(it < CHUNKS)
        def _():
            s = it

            @pl.when(s + AHEAD == 4)
            def _():
                second_here(1)

            arrived(blocks(4, 512), recv_hop.at[s])
            for par in range(2):
                @pl.when((s % 2 == par) & (s < CHUNKS - 1))
                def _():
                    forward(s, par)

                @pl.when(((s + AHEAD) % 2 == par) & (s + AHEAD < CHUNKS))
                def _():
                    hop(s + AHEAD, par)

            @pl.when(s == CHUNKS - 2)
            def _():
                for axis, ref in third(CHUNKS - 1, 1, 0):
                    push(ref, along(axis, 2), send_far.at[0], recv_far.at[0])

        @pl.when(it >= LAG_A)
        def _():
            second_round(it - LAG_A)

        @pl.when((it >= LAG_L) & (it < CHUNKS + LAG_L))
        def _():
            s = it - LAG_L
            @pl.when(s < CHUNKS - 1)
            def _():
                arrived(blocks(2, 512), recv_fwd.at[s])

            @pl.when(s == CHUNKS - 1)
            def _():
                arrived(blocks(2, 512), recv_far.at[0])

            logits_of(s)
            for k in range(1, 8):
                push(stat_a.at[s, slot_a], peer_a(k), send_a.at[s], recv_a.at[s])

            @pl.when(s >= CHUNKS - SHARED)
            def _():
                k = s - (CHUNKS - SHARED)
                for xx in range(2):
                    push(grid.at[s // 4, (s // 2) % 2, s % 2, xx], sibling, send_rows.at[k], recv_rows.at[k], dst=far_rows.at[k, pl.ds(4 * xx, 4)])
                push(expo.at[s, pl.ds(0, 256)], sibling, send_expo.at[k], recv_expo.at[k], dst=far_expo.at[k])

    @pl.loop(0, 12)
    def _(j):
        half = jnp.where((j < 4) | ((j >= 8) & (j < 10)), 0, 1)
        s = jnp.where(j < 4, j, jnp.where(j < 10, j - 4, j - 6))
        due = jnp.where(j == ROUNDS[0], 4, jnp.where(j == ROUNDS[1], 5, jnp.where(j == ROUNDS[2], 6, jnp.where(j == ROUNDS[3], 7, 0))))

        @pl.when(due > 0)
        def _():
            second_round(due)

        @pl.when(half == 0)
        def _():
            weigh(s)

        add_chunk(half, s)

        @pl.when(j == 9)
        def _():
            push(moments.at[0], sibling, send_one.at[11], recv_one.at[11], dst=got_moments)
            push(mass.at[0], sibling, send_one.at[12], recv_one.at[12], dst=got_mass)

    def far_squared(n, xs):
        wide = xs.astype(F32)
        return (wide * wide).astype(BF16)

    @pl.loop(0, SHARED)
    def _(k):
        s = CHUNKS - SHARED + k
        weigh(s)
        push(scales.at[s], sibling, send_scale.at[k], recv_scale.at[k], dst=far_scale.at[k])
        add_chunk(1, s)
        arrived(far_rows.at[k], recv_rows.at[k])
        arrived(far_expo.at[k], recv_expo.at[k])
        arrived(far_scale.at[k], recv_scale.at[k])
        add_half(1, far_expo.at[k], 0, far_scale[k][0:1, :], lambda f: far_rows[k, f], far_squared)

    score_plane = jnp.sum(score_acc[0:1, :], axis=1, keepdims=True)
    score_mine[...] = jnp.concatenate([jnp.broadcast_to(score_plane, (4, LANES)), jnp.broadcast_to(count_plane, (4, LANES))], axis=0)
    push(score_mine, sibling, send_one.at[13], recv_one.at[13], dst=score_got)
    arrived(score_got, recv_one.at[13])
    arrived(got_mass, recv_one.at[12])
    arrived(got_moments, recv_one.at[11])

    sent(blocks(2, 512), send_far.at[0])
    sent(give, send_one.at[0])
    for k in range(SHARED):
        sent(far_rows.at[k], send_rows.at[k])
        sent(far_expo.at[k], send_expo.at[k])
        sent(far_scale.at[k], send_scale.at[k])
    for part_no in range(3):
        sent(first_done[part_no], send_one.at[1 + part_no])
    for k in range(1, 4):
        sent(second_one, send_x.at[k])
    for group in range(2):
        sent(second_done, send_two.at[1, group])
        sent(second_done, send_two.at[2, group])
    sent(weights.at[1], send_one.at[7])
    sent(offsets.at[1], send_one.at[8])
    sent(valids.at[0, pl.ds(0, 3)], send_one.at[9])
    sent(valids.at[0], send_one.at[10])
    sent(moments.at[0], send_one.at[11])
    sent(mass.at[0], send_one.at[12])
    sent(score_mine, send_one.at[13])

    @pl.loop(0, CHUNKS)
    def _(s):
        sent(blocks(4, 512), send_hop.at[s])

        @pl.when(s < CHUNKS - 1)
        def _():
            sent(blocks(2, 512), send_fwd.at[s])

        sent(stat_a.at[s, pl.ds(0, 7)], send_a.at[s])
        sent(stat_b.at[s, pl.ds(0, 7)], send_b.at[s])


def finish(moments, got_moments, mass, got_mass, means, prec, score_mine, score_got,
           out_means, out_vars, out_weights, out_score, stage_means, stage_vars, means_sem, vars_sem):
    both = score_mine[...] + score_got[...]
    count = jnp.maximum(both[4:5, 0:1], 1.0)
    out_score[...] = both[0:1, :] / count
    copies = []
    for block in range(4):
        weights = []
        for tile in range(2):
            rows = pl.ds(block * 64 + tile * 32, 32)
            weight = jnp.sum(mass[1, rows, :] + got_mass[rows, :], axis=1, keepdims=True)
            weights.append(jnp.broadcast_to(weight, (32, LANES)))
            scale = 1.0 / (weight + PRIOR_MASS)
            c = means[rows, :].astype(F32)
            p = prec[rows, :].astype(F32)
            m = (moments[1, rows, 0:1024] + got_moments[rows, 0:1024] + PRIOR_MASS * c) * scale
            stage_means[rows, :] = m
            second = moments[1, rows, 1024:2048] + got_moments[rows, 1024:2048]
            stage_vars[rows, :] = (second + PRIOR_MASS * (1.0 / p + c * c)) * scale - m * m
        rows = pl.ds(block * 64, 64)
        copies.append(pltpu.make_async_copy(stage_means.at[rows], out_means.at[rows], means_sem.at[block]))
        copies.append(pltpu.make_async_copy(stage_vars.at[rows], out_vars.at[rows], vars_sem.at[block]))
        copies[-2].start()
        copies[-1].start()
        weights = jnp.concatenate(weights + weights, axis=0)
        out_weights[block // 2:block // 2 + 1, (block % 2) * 64:(block % 2) * 64 + 64] = jnp.transpose(weights)[0:1, 0:64] / count
    for copy in copies:
        copy.wait()


def functools_sum(items):
    total = items[0]
    for item in items[1:]:
        total = total + item
    return total


def per_device(embeddings, means, precisions, log_weights, valid):
    hbm = pl.BlockSpec(memory_space=pltpu.HBM)
    vmem = pl.BlockSpec(memory_space=pltpu.VMEM)
    dma = pltpu.SemaphoreType.DMA
    found = pl.pallas_call(
        kernel,
        out_shape=(
            pltpu.VMEM((2, 256, 2048), F32),
            pltpu.VMEM((256, 2048), F32),
            pltpu.VMEM((2, 256, LANES), F32),
            pltpu.VMEM((256, LANES), F32),
            pltpu.VMEM((256, 1024), BF16),
            pltpu.VMEM((256, 1024), BF16),
            pltpu.VMEM((8, LANES), F32),
            pltpu.VMEM((8, LANES), F32),
        ),
        in_specs=[hbm] * 5,
        out_specs=[vmem] * 8,
        scratch_shapes=[
            pltpu.VMEM((64, 512), BF16),
            pltpu.VMEM((16, LANES), F32),
            pltpu.VMEM((8, LANES), jnp.int32),
            pltpu.VMEM((64, 512), BF16),
            pltpu.VMEM((2, 2, 2, 2, 4, 512, LANES), BF16),
            pltpu.VMEM((2, 256, 2048), BF16),
            pltpu.VMEM((2, 256, LANES), F32),
            pltpu.VMEM((2, 4, 8, LANES), F32),
            pltpu.VMEM((CHUNKS, 8, 512), F32),
            pltpu.VMEM((CHUNKS, 512, 1024), BF16),
            pltpu.VMEM((CHUNKS, 512, 512), F32),
            pltpu.VMEM((CHUNKS, 8, LANES), F32),
            pltpu.VMEM((CHUNKS, 8, 8, LANES), F32),
            pltpu.VMEM((CHUNKS, 8, 8, LANES), F32),
            pltpu.VMEM((256, 512), BF16),
            pltpu.VMEM((SHARED, 8, 512, LANES), BF16),
            pltpu.VMEM((SHARED, 256, 512), F32),
            pltpu.VMEM((CHUNKS, 8, 512), F32),
            pltpu.VMEM((SHARED, 8, 512), F32),
            pltpu.VMEM((8, 512), F32),
            dma((5,)),
            dma((17,)), dma((17,)),
            dma((3, 2)), dma((3, 2)),
            dma((4,)), dma((4,)),
            dma((SHARED,)), dma((SHARED,)), dma((SHARED,)), dma((SHARED,)), dma((SHARED,)), dma((SHARED,)),
            dma((1,)), dma((1,)),
            dma((CHUNKS,)), dma((CHUNKS,)),
            dma((CHUNKS,)), dma((CHUNKS,)),
            dma((CHUNKS,)), dma((CHUNKS,)),
            dma((CHUNKS,)), dma((CHUNKS,)),
        ],
        compiler_params=pltpu.CompilerParams(
            collective_id=0, has_side_effects=True, vmem_limit_bytes=50 << 20
        ),
        cost_estimate=pl.CostEstimate(flops=17 << 30, bytes_accessed=8 << 20, transcendentals=4 << 20),
        name="mixture_step",
    )(embeddings.T, means, precisions, log_weights.reshape(16, LANES), valid.reshape(8, LANES))
    found = [pltpu.with_memory_space_constraint(a, pltpu.VMEM) for a in found]
    new_means, new_vars, weights, score = pl.pallas_call(
        finish,
        out_shape=(
            jax.ShapeDtypeStruct((256, 1024), F32),
            jax.ShapeDtypeStruct((256, 1024), F32),
            jax.ShapeDtypeStruct((2, LANES), F32),
            jax.ShapeDtypeStruct((1, LANES), F32),
        ),
        in_specs=[vmem] * 8,
        out_specs=[hbm, hbm, vmem, vmem],
        scratch_shapes=[pltpu.VMEM((256, 1024), F32), pltpu.VMEM((256, 1024), F32), dma((4,)), dma((4,))],
        compiler_params=pltpu.CompilerParams(vmem_limit_bytes=8 << 20),
        cost_estimate=pl.CostEstimate(flops=4 << 20, bytes_accessed=2 << 20, transcendentals=0),
        name="new_parameters",
    )(*found)
    return new_means, new_vars, weights.reshape(256), score[0, 0]


def solution(mesh):
    in_specs = (P("dp", "comp"), P("comp", None), P("comp", None), P("comp"), P("dp"))
    out_specs = (P(("comp", "dp"), None), P(("comp", "dp"), None), P(("comp", "dp")), P())
    return jax.shard_map(
        per_device, mesh=mesh, in_specs=in_specs, out_specs=out_specs, check_vma=False
    )
```

```python
import math

import jax
import jax.numpy as jnp
from jax import lax
from jax.sharding import PartitionSpec as P
import jax.experimental.pallas as pl
import jax.experimental.pallas.tpu as pltpu

PRIOR_MASS = 1.0
MESH = pl.DeviceIdType.MESH
F32, BF16 = jnp.float32, jnp.bfloat16

SIZE = ((32, 96, 96), (48, 80, 80))
BASE = ((0, 128, 320), (0, 192, 352))
FROM_0, FROM_1, FROM_2 = (0, 32, 80, 112), (160, 256), (336, 432)
CHUNKS = 8
AHEAD = 3
SHARED = 2
ROUNDS = (0, 1, 2, 4)
LAG_L, LAG_A = 3, 7
LANES = 128
CONTRACT_LAST = (((1,), (1,)), ((), ()))
CONTRACT = (((1,), (0,)), ((), ()))


def kernel(emb_hbm, means_hbm, prec_hbm, lw_hbm, valid_hbm,
           moments, got_moments, mass, got_mass, means, prec, score_mine, score_got,
           emb, lw_ref, valid_ref, take, grid, weights, offsets, valids, masks,
           squares, expo, peaks, stat_a, stat_b, resp, far_rows, far_squares, far_expo, scales, far_scale, score_acc,
           load_sem, send_one, recv_one, send_two, recv_two, send_x, recv_x, send_rows, recv_rows, send_squares, recv_squares, send_expo, recv_expo, send_scale, recv_scale, send_far, recv_far, send_hop, recv_hop, send_fwd, recv_fwd, send_a, recv_a, send_b, recv_b):
    dp, comp = lax.axis_index("dp"), lax.axis_index("comp")
    xh, y = dp // 4, dp % 4
    xl, z, core = comp // 8, (comp // 2) % 4, comp % 2
    x = xh * 2 + xl
    temper = 0.5 * math.sqrt(1024)

    def dev(x, y, z, core):
        return ((x // 2) * 4 + y, (x % 2) * 8 + z * 2 + core)

    def along(axis, step):
        if axis == "x":
            return dev((x + step) % 4, y, z, core)
        if axis == "y":
            return dev(x, (y + step) % 4, z, core)
        return dev(x, y, (z + step) % 4, core)

    sibling = dev(x, y, z, 1 - core)
    slot_a = x * 2 + y % 2
    slot_b = z * 2 + y // 2

    def peer_a(k):
        to = (slot_a + k) % 8
        return dev(to // 2, (y // 2) * 2 + to % 2, z, core)

    def peer_b(k):
        to = (slot_b + k) % 8
        return dev(x, (to % 2) * 2 + y % 2, to // 2, core)

    def push(ref, to, ssem, rsem, dst=None):
        pltpu.make_async_remote_copy(
            src_ref=ref, dst_ref=ref if dst is None else dst, send_sem=ssem, recv_sem=rsem, device_id=to, device_id_type=MESH
        ).start()

    def arrived(ref, rsem):
        pltpu.make_async_remote_copy(
            src_ref=ref, dst_ref=ref, send_sem=send_one.at[0], recv_sem=rsem, device_id=sibling, device_id_type=MESH
        ).wait_recv()

    def sent(ref, ssem):
        pltpu.make_async_remote_copy(
            src_ref=ref, dst_ref=ref, send_sem=ssem, recv_sem=recv_one.at[0], device_id=sibling, device_id_type=MESH
        ).wait_send()

    own = pl.multiple_of(dp * 256, 256)
    load_emb = pltpu.make_async_copy(emb_hbm.at[:, pl.ds(pl.multiple_of(core * 512, 512), 512)], emb, load_sem.at[0])
    load_means = pltpu.make_async_copy(means_hbm.at[pl.ds(own, 256)], means, load_sem.at[1])
    load_prec = pltpu.make_async_copy(prec_hbm.at[pl.ds(own, 256)], prec, load_sem.at[2])
    load_lw = pltpu.make_async_copy(lw_hbm, lw_ref, load_sem.at[3])
    load_valid = pltpu.make_async_copy(valid_hbm, valid_ref, load_sem.at[4])
    load_emb.start()
    load_valid.start()
    load_lw.start()
    load_means.start()
    load_prec.start()

    barrier = pltpu.get_barrier_semaphore()
    friends = [sibling]
    for k in range(1, 4):
        friends += [along("x", k), along("y", k), along("z", k)]
        friends += []
    for k in range(4):
        if k:
            friends.append(dev((x + k) % 4, (y // 2) * 2 + 1 - y % 2, z, core))
            friends.append(dev(x, (y + 2) % 4, (z + k) % 4, core))
    for friend in friends:
        pl.semaphore_signal(barrier, inc=1, device_id=friend, device_id_type=MESH)
    pl.semaphore_wait(barrier, len(friends))

    give = emb_hbm.at[:, pl.ds(pl.multiple_of((1 - core) * 512, 512), 512)]
    push(give, sibling, send_one.at[0], recv_one.at[0], dst=take)
    load_valid.wait()
    vrow = jnp.where(core == 0, valid_ref[0:4, :], valid_ref[4:8, :]).astype(F32)
    valids[xh, y] = jnp.concatenate([vrow, vrow], axis=0)
    for k in range(1, 4):
        push(valids.at[xh, y], along("y", k), send_one.at[9], recv_one.at[9])
    load_emb.wait()
    arrived(take, recv_one.at[0])
    kept, taken = emb[...], take[...]
    shard = jnp.concatenate([jnp.where(core == 0, kept, taken), jnp.where(core == 0, taken, kept)], axis=0)
    shard = jnp.transpose(shard)
    def rows_of(part, par, index):
        n = SIZE[par][part]
        return pl.ds(pl.multiple_of(BASE[par][part] + index * n, 16), n)

    for par in range(2):
        for jh in range(2):
            at = FROM_0[2 * jh + par]
            grid[xh, jh, par, xl, z, rows_of(0, par, y), :] = shard[at:at + SIZE[par][0]]
        at = FROM_1[par]
        grid[xh, y // 2, par, xl, z, rows_of(1, par, y % 2), :] = shard[at:at + SIZE[par][1]]
        at = FROM_2[par]
        grid[y // 2, y % 2, par, xl, z, rows_of(2, par, xh), :] = shard[at:at + SIZE[par][2]]

    first = []
    for par in range(2):
        first += [
            (0, "z", grid.at[xh, :, par, xl, z, rows_of(0, par, y)]),
            (1, "x", grid.at[xh, y // 2, par, xl, z, rows_of(1, par, y % 2)]),
            (2, "y", grid.at[y // 2, y % 2, par, xl, z, rows_of(2, par, xh)]),
        ]
    for k in range(1, 4):
        for part_no, axis, ref in first:
            push(ref, along(axis, k), send_one.at[1 + part_no], recv_one.at[1 + part_no])

    for par in range(2):
        for k in range(1, 4):
            push(grid.at[xh, :, par, xl, z, rows_of(0, par, y)], along("x", k), send_x.at[k], recv_x.at[k])
            push(grid.at[xh, y // 2, par, xl, z, rows_of(1, par, y % 2)], along("y", k), send_two.at[1, xh], recv_two.at[1, xh])
            push(grid.at[y // 2, y % 2, par, xl, z, rows_of(2, par, xh)], along("z", k), send_two.at[2, y // 2], recv_two.at[2, y // 2])

    load_means.wait()
    load_prec.wait()
    load_lw.wait()
    for tile in range(2):
        row = jnp.broadcast_to(lw_ref[pl.ds(dp * 2 + tile, 1), :], (LANES, LANES))
        offsets[1, tile * LANES:(tile + 1) * LANES, :] = jnp.transpose(row)

    @pl.loop(0, 8)
    def _(t):
        rows = pl.ds(pl.multiple_of(t * 32, 32), 32)
        p = prec[rows, :].astype(F32)
        c = means[rows, :].astype(F32)
        scaled = (p * c).astype(BF16).astype(F32)
        halfp = (0.5 * p).astype(BF16).astype(F32)
        weights[1, rows, 0:1024] = (scaled * (1.0 / temper)).astype(BF16)
        weights[1, rows, 1024:2048] = (halfp * (-1.0 / temper)).astype(BF16)
        both = 0.5 * jnp.sum(jnp.log(p), axis=1, keepdims=True) - 0.5 * jnp.sum(p * c * c, axis=1, keepdims=True)
        offsets[1, rows, :] = (offsets[1, rows, :] + both) * (1.0 / temper)

    push(weights.at[1], sibling, send_one.at[7], recv_one.at[7], dst=weights.at[0])
    push(offsets.at[1], sibling, send_one.at[8], recv_one.at[8], dst=offsets.at[0])

    def blocks(n, rows):
        return grid.at[0, 0, 0, pl.ds(0, n // 4), :, pl.ds(0, rows)] if n % 4 == 0 else grid.at[0, 0, 0, 0, pl.ds(0, n), pl.ds(0, rows)]

    first_done = (blocks(3, 160), blocks(3, 176), blocks(3, 176))
    second_one = blocks(4, 160)
    second_done = blocks(3, 352)

    def second(part_no, group):
        def copies(select):
            for par in range(2):
                for k in range(1, 4):
                    if part_no == 1:
                        push(grid.at[group, y // 2, par, select(xl), z, rows_of(1, par, y % 2)], along("y", k), send_two.at[1, group], recv_two.at[1, group])
                    else:
                        push(grid.at[group, select(y % 2), par, xl, z, rows_of(2, par, xh)], along("z", k), send_two.at[2, group], recv_two.at[2, group])

        mine = xh if part_no == 1 else y // 2

        @pl.when(mine == group)
        def _():
            copies(lambda own: 1 - own)

        @pl.when(mine != group)
        def _():
            copies(lambda own: slice(None))

    def second_rows():
        for par in range(2):
            for k in range(1, 4):
                for other in range(1, 4):
                    push(grid.at[xh, :, par, xl, (z + other) % 4, rows_of(0, par, y)], along("x", k), send_x.at[k], recv_x.at[k])

    def second_here(group):
        for k in range(1, 4):
            @pl.when(((x + 4 - k) % 4) // 2 == group)
            def _():
                arrived(second_one, recv_x.at[k])

        arrived(second_done, recv_two.at[1, group])
        arrived(second_done, recv_two.at[2, group])

    arrived(first_done[0], recv_one.at[1])
    second_rows()
    for part_no in (1, 2):
        arrived(first_done[part_no], recv_one.at[1 + part_no])
        second(part_no, 0)
    for part_no in (1, 2):
        second(part_no, 1)
    arrived(valids.at[0, pl.ds(0, 3)], recv_one.at[9])
    push(valids.at[xh], along("x", 2), send_one.at[10], recv_one.at[10])

    moments[...] = jnp.zeros_like(moments)
    mass[...] = jnp.zeros_like(mass)
    score_acc[...] = jnp.zeros_like(score_acc)

    def third(s, par, step):
        i, jh = s // 4, (s // 2) % 2
        yy, zz, xx = (y + step) % 4, (z + step) % 4, (x + step) % 4
        return (
            ("y", grid.at[i, jh, par, :, :, rows_of(0, par, yy)]),
            ("z", grid.at[i, jh, par, :, zz, pl.ds(BASE[par][1], 2 * SIZE[par][1])]),
            ("x", grid.at[i, jh, par, xx % 2, :, rows_of(2, par, xx // 2)]),
        )

    def hop(s, par):
        for axis, ref in third(s, par, 0):
            for step in (1, 3):
                push(ref, along(axis, step), send_hop.at[s], recv_hop.at[s])

    def forward(s, par):
        i, jh = s // 4, (s // 2) % 2
        for half, step in ((0, 1), (1, 3)):
            yy, zz, xx = (y + 4 - step) % 4, (z + 4 - step) % 4, (x + 4 - step) % 4
            for axis, ref in (
                ("y", grid.at[i, jh, par, half, :, rows_of(0, par, yy)]),
                ("z", grid.at[i, jh, par, half, zz, pl.ds(BASE[par][1], 2 * SIZE[par][1])]),
                ("x", grid.at[i, jh, par, xx % 2, pl.ds(2 * half, 2), rows_of(2, par, xx // 2)]),
            ):
                push(ref, along(axis, step), send_fwd.at[s], recv_fwd.at[s])

    second_here(0)
    for s in range(AHEAD):
        hop(s, s % 2)

    arrived(valids.at[0], recv_one.at[10])
    place = lax.broadcasted_iota(jnp.int32, (8, 512), 1)

    def lanes_of(block):
        v = valids[block // 4, block % 4]
        return jnp.broadcast_to(jnp.concatenate([v[i:i + 1, :] for i in range(4)], axis=1), (8, 512))

    by_block = [lanes_of(b) for b in range(8)]
    count_plane = functools_sum([jnp.sum(b[0:1, :], axis=1, keepdims=True) for b in by_block])
    for s in range(CHUNKS):
        par = s % 2
        n0, n1, n2 = SIZE[par]
        b0, b1, b2 = BASE[par]
        out = by_block[s]
        for yy in range(4):
            moved = pltpu.roll(by_block[(s // 4) * 4 + yy], (yy * n0 - FROM_0[s % 4]) % 512, 1)
            out = jnp.where((place >= yy * n0) & (place < (yy + 1) * n0), moved, out)
        for k in range(2):
            at = b1 + k * n1
            moved = pltpu.roll(by_block[(s // 2) * 2 + k], (at - FROM_1[par]) % 512, 1)
            out = jnp.where((place >= at) & (place < at + n1), moved, out)
            at = b2 + k * n2
            moved = pltpu.roll(by_block[k * 4 + s // 2], (at - FROM_2[par]) % 512, 1)
            out = jnp.where((place >= at) & (place < at + n2), moved, out)
        masks[s] = out

    arrived(weights.at[0], recv_one.at[7])
    arrived(offsets.at[0], recv_one.at[8])

    def logits_of(s):
        chunk, slot = grid.at[s // 4, (s // 2) % 2, s % 2], s
        tops, sums = [], []
        for n in range(2):
            rows = pl.ds(n * 256, 256)
            xs = jnp.concatenate([chunk[f // 4, f % 4, rows, :] for f in range(8)], axis=1)
            wide = xs.astype(F32)
            sq = (wide * wide).astype(BF16)
            squares[slot, rows, :] = sq
            w = weights[...].reshape(512, 2048)
            l = lax.dot_general(w[:, 0:1024], xs, CONTRACT_LAST, preferred_element_type=F32)
            l = l + lax.dot_general(w[:, 1024:2048], sq, CONTRACT_LAST, preferred_element_type=F32)
            off = offsets[...].reshape(512, LANES)
            l = l + jnp.concatenate([off, off], axis=1)
            top = jnp.max(l, axis=0, keepdims=True)
            e = jnp.exp(l - top)
            expo[slot, :, rows] = e
            total = jnp.sum(e, axis=0, keepdims=True)
            tops += [top[:, 0:128], top[:, 128:256]]
            sums += [total[:, 0:128], total[:, 128:256]]
        stat = jnp.concatenate(tops + sums, axis=0)
        stat_a[s, slot_a] = stat
        peaks[slot] = stat

    def combine(ref):
        both = [ref[k] for k in range(8)]
        top = both[0][0:4]
        for b in both[1:]:
            top = jnp.maximum(top, b[0:4])
        total = jnp.zeros_like(top)
        for b in both:
            total = total + b[4:8] * jnp.exp(b[0:4] - top)
        return top, total

    def add(low, count, e_ref, e_low, weight, features, squared):
        for at in range(0, count, 128):
            r = (e_ref[pl.ds(e_low + at, 128), :] * weight).astype(BF16)
            resp[pl.ds(at, 128), :] = r
            wide = r.astype(F32)
            mass[pl.ds(low + at, 128), :] += wide[:, 0:128] + wide[:, 128:256] + wide[:, 256:384] + wide[:, 384:512]
        r = resp[pl.ds(0, count), :]
        into = pl.ds(low, count)
        for n in range(4):
            xs = jnp.concatenate([features(2 * n), features(2 * n + 1)], axis=1)
            moments[into, n * 256:(n + 1) * 256] += lax.dot_general(r, xs, CONTRACT, preferred_element_type=F32)
            sq = squared(n)
            moments[into, 1024 + n * 256:1024 + (n + 1) * 256] += lax.dot_general(r, sq, CONTRACT, preferred_element_type=F32)

    def second_round(s):
        arrived(stat_a.at[s, pl.ds(0, 7)], recv_a.at[s])
        top, total = combine(stat_a.at[s])
        stat_b[s, slot_b] = jnp.concatenate([top, total], axis=0)
        for k in range(1, 8):
            push(stat_b.at[s, slot_b], peer_b(k), send_b.at[s], recv_b.at[s])

    def weigh(s):
        arrived(stat_b.at[s, pl.ds(0, 7)], recv_b.at[s])
        top, total = combine(stat_b.at[s])
        log_total = top + jnp.log(total)
        mask = masks[s][0:1, :]
        scale = jnp.exp(peaks[s][0:4] - log_total)
        scale = jnp.concatenate([scale[k:k + 1, :] for k in range(4)], axis=1) * mask
        score = jnp.concatenate([log_total[k:k + 1, :] for k in range(4)], axis=1) * mask
        score_acc[0:1, :] += score
        scales[s] = jnp.broadcast_to(scale, (8, 512))

    def add_chunk(s, low):
        chunk = grid.at[s // 4, (s // 2) % 2, s % 2]
        add(low, 512 - low, expo.at[s], low, scales[s][0:1, :], lambda f: chunk[f // 4, f % 4],
            lambda n: squares[s, :, n * 256:(n + 1) * 256])

    @pl.loop(0, CHUNKS + LAG_L)
    def _(it):
        @pl.when(it < CHUNKS)
        def _():
            s = it

            @pl.when(s + AHEAD == 4)
            def _():
                second_here(1)

            arrived(blocks(4, 512), recv_hop.at[s])
            for par in range(2):
                @pl.when((s % 2 == par) & (s < CHUNKS - 1))
                def _():
                    forward(s, par)

                @pl.when(((s + AHEAD) % 2 == par) & (s + AHEAD < CHUNKS))
                def _():
                    hop(s + AHEAD, par)

            @pl.when(s == CHUNKS - 2)
            def _():
                for axis, ref in third(CHUNKS - 1, 1, 0):
                    push(ref, along(axis, 2), send_far.at[0], recv_far.at[0])

        @pl.when(it >= LAG_A)
        def _():
            second_round(it - LAG_A)

        @pl.when((it >= LAG_L) & (it < CHUNKS + LAG_L))
        def _():
            s = it - LAG_L
            @pl.when(s < CHUNKS - 1)
            def _():
                arrived(blocks(2, 512), recv_fwd.at[s])

            @pl.when(s == CHUNKS - 1)
            def _():
                arrived(blocks(2, 512), recv_far.at[0])

            logits_of(s)
            for k in range(1, 8):
                push(stat_a.at[s, slot_a], peer_a(k), send_a.at[s], recv_a.at[s])

            @pl.when(s >= CHUNKS - SHARED)
            def _():
                k = s - (CHUNKS - SHARED)
                for xx in range(2):
                    push(grid.at[s // 4, (s // 2) % 2, s % 2, xx], sibling, send_rows.at[k], recv_rows.at[k], dst=far_rows.at[k, pl.ds(4 * xx, 4)])
                push(squares.at[s], sibling, send_squares.at[k], recv_squares.at[k], dst=far_squares.at[k])
                push(expo.at[s, pl.ds(0, 256)], sibling, send_expo.at[k], recv_expo.at[k], dst=far_expo.at[k])

    @pl.loop(0, CHUNKS - SHARED)
    def _(s):
        due = jnp.where(s == ROUNDS[0], 4, jnp.where(s == ROUNDS[1], 5, jnp.where(s == ROUNDS[2], 6, jnp.where(s == ROUNDS[3], 7, 0))))

        @pl.when(due > 0)
        def _():
            second_round(due)

        weigh(s)
        add_chunk(s, 0)

    push(moments.at[pl.ds(0, 256)], sibling, send_one.at[11], recv_one.at[11], dst=got_moments)
    push(mass.at[pl.ds(0, 256)], sibling, send_one.at[12], recv_one.at[12], dst=got_mass)

    sent(give, send_one.at[0])
    for part_no in range(3):
        sent(first_done[part_no], send_one.at[1 + part_no])
    for k in range(1, 4):
        sent(second_one, send_x.at[k])
    for group in range(2):
        sent(second_done, send_two.at[1, group])
        sent(second_done, send_two.at[2, group])
    sent(weights.at[1], send_one.at[7])
    sent(offsets.at[1], send_one.at[8])
    sent(valids.at[0, pl.ds(0, 3)], send_one.at[9])
    sent(valids.at[0], send_one.at[10])
    sent(blocks(2, 512), send_far.at[0])

    @pl.loop(0, CHUNKS)
    def _(s):
        sent(blocks(4, 512), send_hop.at[s])
        sent(stat_a.at[s, pl.ds(0, 7)], send_a.at[s])

        @pl.when(s < CHUNKS - 1)
        def _():
            sent(blocks(2, 512), send_fwd.at[s])

    @pl.loop(0, SHARED)
    def _(k):
        s = CHUNKS - SHARED + k
        weigh(s)
        push(scales.at[s], sibling, send_scale.at[k], recv_scale.at[k], dst=far_scale.at[k])

        @pl.when(k == SHARED - 1)
        def _():
            score_plane = jnp.sum(score_acc[0:1, :], axis=1, keepdims=True)
            score_mine[...] = jnp.concatenate([jnp.broadcast_to(score_plane, (4, LANES)), jnp.broadcast_to(count_plane, (4, LANES))], axis=0)
            push(score_mine, sibling, send_one.at[13], recv_one.at[13], dst=score_got)

        add_chunk(s, 256)
        arrived(far_rows.at[k], recv_rows.at[k])
        arrived(far_squares.at[k], recv_squares.at[k])
        arrived(far_expo.at[k], recv_expo.at[k])
        arrived(far_scale.at[k], recv_scale.at[k])
        add(256, 256, far_expo.at[k], 0, far_scale[k][0:1, :], lambda f: far_rows[k, f],
            lambda n: far_squares[k, :, n * 256:(n + 1) * 256])

    arrived(score_got, recv_one.at[13])
    arrived(got_mass, recv_one.at[12])
    arrived(got_moments, recv_one.at[11])

    sent(got_moments, send_one.at[11])
    sent(got_mass, send_one.at[12])
    sent(score_mine, send_one.at[13])
    for k in range(SHARED):
        sent(far_rows.at[k], send_rows.at[k])
        sent(far_squares.at[k], send_squares.at[k])
        sent(far_expo.at[k], send_expo.at[k])
        sent(far_scale.at[k], send_scale.at[k])

    @pl.loop(0, CHUNKS)
    def _(s):
        sent(stat_b.at[s, pl.ds(0, 7)], send_b.at[s])


def finish(moments, got_moments, mass, got_mass, means, prec, score_mine, score_got,
           out_means, out_vars, out_weights, out_score, stage_means, stage_vars, means_sem, vars_sem):
    both = score_mine[...] + score_got[...]
    count = jnp.maximum(both[4:5, 0:1], 1.0)
    out_score[...] = both[0:1, :] / count
    copies = []
    for block in range(4):
        weights = []
        for tile in range(2):
            rows = pl.ds(block * 64 + tile * 32, 32)
            own = pl.ds(256 + block * 64 + tile * 32, 32)
            weight = jnp.sum(mass[own, :] + got_mass[rows, :], axis=1, keepdims=True)
            weights.append(jnp.broadcast_to(weight, (32, LANES)))
            scale = 1.0 / (weight + PRIOR_MASS)
            c = means[rows, :].astype(F32)
            p = prec[rows, :].astype(F32)
            m = (moments[own, 0:1024] + got_moments[rows, 0:1024] + PRIOR_MASS * c) * scale
            stage_means[rows, :] = m
            second = moments[own, 1024:2048] + got_moments[rows, 1024:2048]
            stage_vars[rows, :] = (second + PRIOR_MASS * (1.0 / p + c * c)) * scale - m * m
        rows = pl.ds(block * 64, 64)
        copies.append(pltpu.make_async_copy(stage_means.at[rows], out_means.at[rows], means_sem.at[block]))
        copies.append(pltpu.make_async_copy(stage_vars.at[rows], out_vars.at[rows], vars_sem.at[block]))
        copies[-2].start()
        copies[-1].start()
        weights = jnp.concatenate(weights + weights, axis=0)
        out_weights[block // 2:block // 2 + 1, (block % 2) * 64:(block % 2) * 64 + 64] = jnp.transpose(weights)[0:1, 0:64] / count
    for copy in copies:
        copy.wait()


def functools_sum(items):
    total = items[0]
    for item in items[1:]:
        total = total + item
    return total


def per_device(embeddings, means, precisions, log_weights, valid):
    hbm = pl.BlockSpec(memory_space=pltpu.HBM)
    vmem = pl.BlockSpec(memory_space=pltpu.VMEM)
    dma = pltpu.SemaphoreType.DMA
    found = pl.pallas_call(
        kernel,
        out_shape=(
            pltpu.VMEM((512, 2048), F32),
            pltpu.VMEM((256, 2048), F32),
            pltpu.VMEM((512, LANES), F32),
            pltpu.VMEM((256, LANES), F32),
            pltpu.VMEM((256, 1024), BF16),
            pltpu.VMEM((256, 1024), BF16),
            pltpu.VMEM((8, LANES), F32),
            pltpu.VMEM((8, LANES), F32),
        ),
        in_specs=[hbm] * 5,
        out_specs=[vmem] * 8,
        scratch_shapes=[
            pltpu.VMEM((64, 512), BF16),
            pltpu.VMEM((16, LANES), F32),
            pltpu.VMEM((8, LANES), jnp.int32),
            pltpu.VMEM((64, 512), BF16),
            pltpu.VMEM((2, 2, 2, 2, 4, 512, LANES), BF16),
            pltpu.VMEM((2, 256, 2048), BF16),
            pltpu.VMEM((2, 256, LANES), F32),
            pltpu.VMEM((2, 4, 8, LANES), F32),
            pltpu.VMEM((CHUNKS, 8, 512), F32),
            pltpu.VMEM((CHUNKS, 512, 1024), BF16),
            pltpu.VMEM((CHUNKS, 512, 512), F32),
            pltpu.VMEM((CHUNKS, 8, LANES), F32),
            pltpu.VMEM((CHUNKS, 8, 8, LANES), F32),
            pltpu.VMEM((CHUNKS, 8, 8, LANES), F32),
            pltpu.VMEM((512, 512), BF16),
            pltpu.VMEM((SHARED, 8, 512, LANES), BF16),
            pltpu.VMEM((SHARED, 512, 1024), BF16),
            pltpu.VMEM((SHARED, 256, 512), F32),
            pltpu.VMEM((CHUNKS, 8, 512), F32),
            pltpu.VMEM((SHARED, 8, 512), F32),
            pltpu.VMEM((8, 512), F32),
            dma((5,)),
            dma((17,)), dma((17,)),
            dma((3, 2)), dma((3, 2)),
            dma((4,)), dma((4,)),
            dma((SHARED,)), dma((SHARED,)), dma((SHARED,)), dma((SHARED,)),
            dma((SHARED,)), dma((SHARED,)), dma((SHARED,)), dma((SHARED,)),
            dma((1,)), dma((1,)),
            dma((CHUNKS,)), dma((CHUNKS,)),
            dma((CHUNKS,)), dma((CHUNKS,)),
            dma((CHUNKS,)), dma((CHUNKS,)),
            dma((CHUNKS,)), dma((CHUNKS,)),
        ],
        compiler_params=pltpu.CompilerParams(
            collective_id=0, has_side_effects=True, vmem_limit_bytes=50 << 20
        ),
        cost_estimate=pl.CostEstimate(flops=17 << 30, bytes_accessed=8 << 20, transcendentals=4 << 20),
        name="mixture_step",
    )(embeddings.T, means, precisions, log_weights.reshape(16, LANES), valid.reshape(8, LANES))
    found = [pltpu.with_memory_space_constraint(a, pltpu.VMEM) for a in found]
    new_means, new_vars, weights, score = pl.pallas_call(
        finish,
        out_shape=(
            jax.ShapeDtypeStruct((256, 1024), F32),
            jax.ShapeDtypeStruct((256, 1024), F32),
            jax.ShapeDtypeStruct((2, LANES), F32),
            jax.ShapeDtypeStruct((1, LANES), F32),
        ),
        in_specs=[vmem] * 8,
        out_specs=[hbm, hbm, vmem, vmem],
        scratch_shapes=[pltpu.VMEM((256, 1024), F32), pltpu.VMEM((256, 1024), F32), dma((4,)), dma((4,))],
        compiler_params=pltpu.CompilerParams(vmem_limit_bytes=8 << 20),
        cost_estimate=pl.CostEstimate(flops=4 << 20, bytes_accessed=2 << 20, transcendentals=0),
        name="new_parameters",
    )(*found)
    return new_means, new_vars, weights.reshape(256), score[0, 0]


def solution(mesh):
    in_specs = (P("dp", "comp"), P("comp", None), P("comp", None), P("comp"), P("dp"))
    out_specs = (P(("comp", "dp"), None), P(("comp", "dp"), None), P(("comp", "dp")), P())
    return jax.shard_map(
        per_device, mesh=mesh, in_specs=in_specs, out_specs=out_specs, check_vma=False
    )
```

```python
import math

import jax
import jax.numpy as jnp
from jax import lax
from jax.sharding import PartitionSpec as P
import jax.experimental.pallas as pl
import jax.experimental.pallas.tpu as pltpu

PRIOR_MASS = 1.0
MESH = pl.DeviceIdType.MESH
F32, BF16 = jnp.float32, jnp.bfloat16

SIZE = ((32, 96, 96), (48, 80, 80))
BASE = ((0, 128, 320), (0, 192, 352))
FROM_0, FROM_1, FROM_2 = (0, 32, 80, 112), (160, 256), (336, 432)
CHUNKS = 8
AHEAD = 3
SHARED = 1
ROUNDS = (0, 1, 2, 4)
LAG_L, LAG_A = 3, 7
LANES = 128
CONTRACT_LAST = (((1,), (1,)), ((), ()))
CONTRACT = (((1,), (0,)), ((), ()))


def kernel(emb_hbm, means_hbm, prec_hbm, lw_hbm, valid_hbm,
           moments, got_moments, mass, got_mass, means, prec, score_mine, score_got,
           emb, lw_ref, valid_ref, take, grid, weights, offsets, valids, masks,
           squares, expo, peaks, stat_a, stat_b, resp, far_rows, far_squares, far_expo, scales, far_scale, score_acc,
           load_sem, send_one, recv_one, send_two, recv_two, send_x, recv_x, send_rows, recv_rows, send_squares, recv_squares, send_expo, recv_expo, send_scale, recv_scale, send_far, recv_far, send_hop, recv_hop, send_fwd, recv_fwd, send_a, recv_a, send_b, recv_b):
    dp, comp = lax.axis_index("dp"), lax.axis_index("comp")
    xh, y = dp // 4, dp % 4
    xl, z, core = comp // 8, (comp // 2) % 4, comp % 2
    x = xh * 2 + xl
    temper = 0.5 * math.sqrt(1024)

    def dev(x, y, z, core):
        return ((x // 2) * 4 + y, (x % 2) * 8 + z * 2 + core)

    def along(axis, step):
        if axis == "x":
            return dev((x + step) % 4, y, z, core)
        if axis == "y":
            return dev(x, (y + step) % 4, z, core)
        return dev(x, y, (z + step) % 4, core)

    sibling = dev(x, y, z, 1 - core)
    slot_a = x * 2 + y % 2
    slot_b = z * 2 + y // 2

    def peer_a(k):
        to = (slot_a + k) % 8
        return dev(to // 2, (y // 2) * 2 + to % 2, z, core)

    def peer_b(k):
        to = (slot_b + k) % 8
        return dev(x, (to % 2) * 2 + y % 2, to // 2, core)

    def push(ref, to, ssem, rsem, dst=None):
        pltpu.make_async_remote_copy(
            src_ref=ref, dst_ref=ref if dst is None else dst, send_sem=ssem, recv_sem=rsem, device_id=to, device_id_type=MESH
        ).start()

    def arrived(ref, rsem):
        pltpu.make_async_remote_copy(
            src_ref=ref, dst_ref=ref, send_sem=send_one.at[0], recv_sem=rsem, device_id=sibling, device_id_type=MESH
        ).wait_recv()

    def sent(ref, ssem):
        pltpu.make_async_remote_copy(
            src_ref=ref, dst_ref=ref, send_sem=ssem, recv_sem=recv_one.at[0], device_id=sibling, device_id_type=MESH
        ).wait_send()

    own = pl.multiple_of(dp * 256, 256)
    load_emb = pltpu.make_async_copy(emb_hbm, emb, load_sem.at[0])
    load_means = pltpu.make_async_copy(means_hbm.at[pl.ds(own, 256)], means, load_sem.at[1])
    load_prec = pltpu.make_async_copy(prec_hbm.at[pl.ds(own, 256)], prec, load_sem.at[2])
    load_lw = pltpu.make_async_copy(lw_hbm, lw_ref, load_sem.at[3])
    load_valid = pltpu.make_async_copy(valid_hbm, valid_ref, load_sem.at[4])
    load_emb.start()
    load_valid.start()
    load_lw.start()
    load_means.start()
    load_prec.start()

    barrier = pltpu.get_barrier_semaphore()
    friends = [sibling]
    for k in range(1, 4):
        friends += [along("x", k), along("y", k), along("z", k)]
        friends += []
    for k in range(4):
        if k:
            friends.append(dev((x + k) % 4, (y // 2) * 2 + 1 - y % 2, z, core))
            friends.append(dev(x, (y + 2) % 4, (z + k) % 4, core))
    for friend in friends:
        pl.semaphore_signal(barrier, inc=1, device_id=friend, device_id_type=MESH)
    pl.semaphore_wait(barrier, len(friends))

    load_emb.wait()
    give = emb.at[:, pl.ds(pl.multiple_of((1 - core) * 512, 512), 512)]
    push(give, sibling, send_one.at[0], recv_one.at[0], dst=take)
    load_valid.wait()
    vrow = jnp.where(core == 0, valid_ref[0:4, :], valid_ref[4:8, :]).astype(F32)
    valids[xh, y] = jnp.concatenate([vrow, vrow], axis=0)
    for k in range(1, 4):
        push(valids.at[xh, y], along("y", k), send_one.at[9], recv_one.at[9])
    kept = emb[:, pl.ds(pl.multiple_of(core * 512, 512), 512)]
    arrived(take, recv_one.at[0])
    taken = take[...]
    shard = jnp.concatenate([jnp.where(core == 0, kept, taken), jnp.where(core == 0, taken, kept)], axis=0)
    shard = jnp.transpose(shard)
    def rows_of(part, par, index):
        n = SIZE[par][part]
        return pl.ds(pl.multiple_of(BASE[par][part] + index * n, 16), n)

    for par in range(2):
        for jh in range(2):
            at = FROM_0[2 * jh + par]
            grid[xh, jh, par, xl, z, rows_of(0, par, y), :] = shard[at:at + SIZE[par][0]]
        at = FROM_1[par]
        grid[xh, y // 2, par, xl, z, rows_of(1, par, y % 2), :] = shard[at:at + SIZE[par][1]]
        at = FROM_2[par]
        grid[y // 2, y % 2, par, xl, z, rows_of(2, par, xh), :] = shard[at:at + SIZE[par][2]]

    first = []
    for par in range(2):
        first += [
            (0, "z", grid.at[xh, :, par, xl, z, rows_of(0, par, y)]),
            (1, "x", grid.at[xh, y // 2, par, xl, z, rows_of(1, par, y % 2)]),
            (2, "y", grid.at[y // 2, y % 2, par, xl, z, rows_of(2, par, xh)]),
        ]
    for k in range(1, 4):
        for part_no, axis, ref in first:
            push(ref, along(axis, k), send_one.at[1 + part_no], recv_one.at[1 + part_no])

    for par in range(2):
        for k in range(1, 4):
            push(grid.at[xh, :, par, xl, z, rows_of(0, par, y)], along("x", k), send_x.at[k], recv_x.at[k])
            push(grid.at[xh, y // 2, par, xl, z, rows_of(1, par, y % 2)], along("y", k), send_two.at[1, xh], recv_two.at[1, xh])
            push(grid.at[y // 2, y % 2, par, xl, z, rows_of(2, par, xh)], along("z", k), send_two.at[2, y // 2], recv_two.at[2, y // 2])

    load_means.wait()
    load_prec.wait()
    load_lw.wait()
    for tile in range(2):
        row = jnp.broadcast_to(lw_ref[pl.ds(dp * 2 + tile, 1), :], (LANES, LANES))
        offsets[1, tile * LANES:(tile + 1) * LANES, :] = jnp.transpose(row)

    @pl.loop(0, 8)
    def _(t):
        rows = pl.ds(pl.multiple_of(t * 32, 32), 32)
        p = prec[rows, :].astype(F32)
        c = means[rows, :].astype(F32)
        scaled = (p * c).astype(BF16).astype(F32)
        halfp = (0.5 * p).astype(BF16).astype(F32)
        weights[1, rows, 0:1024] = (scaled * (1.0 / temper)).astype(BF16)
        weights[1, rows, 1024:2048] = (halfp * (-1.0 / temper)).astype(BF16)
        both = 0.5 * jnp.sum(jnp.log(p), axis=1, keepdims=True) - 0.5 * jnp.sum(p * c * c, axis=1, keepdims=True)
        offsets[1, rows, :] = (offsets[1, rows, :] + both) * (1.0 / temper)

    push(weights.at[1], sibling, send_one.at[7], recv_one.at[7], dst=weights.at[0])
    push(offsets.at[1], sibling, send_one.at[8], recv_one.at[8], dst=offsets.at[0])

    def blocks(n, rows):
        return grid.at[0, 0, 0, pl.ds(0, n // 4), :, pl.ds(0, rows)] if n % 4 == 0 else grid.at[0, 0, 0, 0, pl.ds(0, n), pl.ds(0, rows)]

    first_done = (blocks(3, 160), blocks(3, 176), blocks(3, 176))
    second_one = blocks(4, 160)
    second_done = blocks(3, 352)

    def second(part_no, group):
        def copies(select):
            for par in range(2):
                for k in range(1, 4):
                    if part_no == 1:
                        push(grid.at[group, y // 2, par, select(xl), z, rows_of(1, par, y % 2)], along("y", k), send_two.at[1, group], recv_two.at[1, group])
                    else:
                        push(grid.at[group, select(y % 2), par, xl, z, rows_of(2, par, xh)], along("z", k), send_two.at[2, group], recv_two.at[2, group])

        mine = xh if part_no == 1 else y // 2

        @pl.when(mine == group)
        def _():
            copies(lambda own: 1 - own)

        @pl.when(mine != group)
        def _():
            copies(lambda own: slice(None))

    def second_rows():
        for par in range(2):
            for k in range(1, 4):
                for other in range(1, 4):
                    push(grid.at[xh, :, par, xl, (z + other) % 4, rows_of(0, par, y)], along("x", k), send_x.at[k], recv_x.at[k])

    def second_here(group):
        for k in range(1, 4):
            @pl.when(((x + 4 - k) % 4) // 2 == group)
            def _():
                arrived(second_one, recv_x.at[k])

        arrived(second_done, recv_two.at[1, group])
        arrived(second_done, recv_two.at[2, group])

    arrived(first_done[0], recv_one.at[1])
    second_rows()
    for part_no in (1, 2):
        arrived(first_done[part_no], recv_one.at[1 + part_no])
        second(part_no, 0)
    for part_no in (1, 2):
        second(part_no, 1)
    arrived(valids.at[0, pl.ds(0, 3)], recv_one.at[9])
    push(valids.at[xh], along("x", 2), send_one.at[10], recv_one.at[10])

    moments[...] = jnp.zeros_like(moments)
    mass[...] = jnp.zeros_like(mass)
    score_acc[...] = jnp.zeros_like(score_acc)

    def third(s, par, step):
        i, jh = s // 4, (s // 2) % 2
        yy, zz, xx = (y + step) % 4, (z + step) % 4, (x + step) % 4
        return (
            ("y", grid.at[i, jh, par, :, :, rows_of(0, par, yy)]),
            ("z", grid.at[i, jh, par, :, zz, pl.ds(BASE[par][1], 2 * SIZE[par][1])]),
            ("x", grid.at[i, jh, par, xx % 2, :, rows_of(2, par, xx // 2)]),
        )

    def hop(s, par):
        for axis, ref in third(s, par, 0):
            for step in (1, 3):
                push(ref, along(axis, step), send_hop.at[s], recv_hop.at[s])

    def forward(s, par):
        i, jh = s // 4, (s // 2) % 2
        for half, step in ((0, 1), (1, 3)):
            yy, zz, xx = (y + 4 - step) % 4, (z + 4 - step) % 4, (x + 4 - step) % 4
            for axis, ref in (
                ("y", grid.at[i, jh, par, half, :, rows_of(0, par, yy)]),
                ("z", grid.at[i, jh, par, half, zz, pl.ds(BASE[par][1], 2 * SIZE[par][1])]),
                ("x", grid.at[i, jh, par, xx % 2, pl.ds(2 * half, 2), rows_of(2, par, xx // 2)]),
            ):
                push(ref, along(axis, step), send_fwd.at[s], recv_fwd.at[s])

    second_here(0)
    for s in range(AHEAD):
        hop(s, s % 2)

    arrived(valids.at[0], recv_one.at[10])
    place = lax.broadcasted_iota(jnp.int32, (8, 512), 1)

    def lanes_of(block):
        v = valids[block // 4, block % 4]
        return jnp.broadcast_to(jnp.concatenate([v[i:i + 1, :] for i in range(4)], axis=1), (8, 512))

    by_block = [lanes_of(b) for b in range(8)]
    count_plane = functools_sum([jnp.sum(b[0:1, :], axis=1, keepdims=True) for b in by_block])
    for s in range(CHUNKS):
        par = s % 2
        n0, n1, n2 = SIZE[par]
        b0, b1, b2 = BASE[par]
        out = by_block[s]
        for yy in range(4):
            moved = pltpu.roll(by_block[(s // 4) * 4 + yy], (yy * n0 - FROM_0[s % 4]) % 512, 1)
            out = jnp.where((place >= yy * n0) & (place < (yy + 1) * n0), moved, out)
        for k in range(2):
            at = b1 + k * n1
            moved = pltpu.roll(by_block[(s // 2) * 2 + k], (at - FROM_1[par]) % 512, 1)
            out = jnp.where((place >= at) & (place < at + n1), moved, out)
            at = b2 + k * n2
            moved = pltpu.roll(by_block[k * 4 + s // 2], (at - FROM_2[par]) % 512, 1)
            out = jnp.where((place >= at) & (place < at + n2), moved, out)
        masks[s] = out

    arrived(weights.at[0], recv_one.at[7])
    arrived(offsets.at[0], recv_one.at[8])

    def logits_of(s):
        chunk, slot = grid.at[s // 4, (s // 2) % 2, s % 2], s
        tops, sums = [], []
        for n in range(2):
            rows = pl.ds(n * 256, 256)
            xs = jnp.concatenate([chunk[f // 4, f % 4, rows, :] for f in range(8)], axis=1)
            wide = xs.astype(F32)
            sq = (wide * wide).astype(BF16)
            squares[slot, rows, :] = sq
            w = weights[...].reshape(512, 2048)
            l = lax.dot_general(w[:, 0:1024], xs, CONTRACT_LAST, preferred_element_type=F32)
            l = l + lax.dot_general(w[:, 1024:2048], sq, CONTRACT_LAST, preferred_element_type=F32)
            off = offsets[...].reshape(512, LANES)
            l = l + jnp.concatenate([off, off], axis=1)
            top = jnp.max(l, axis=0, keepdims=True)
            e = jnp.exp(l - top)
            expo[slot, :, rows] = e
            total = jnp.sum(e, axis=0, keepdims=True)
            tops += [top[:, 0:128], top[:, 128:256]]
            sums += [total[:, 0:128], total[:, 128:256]]
        stat = jnp.concatenate(tops + sums, axis=0)
        stat_a[s, slot_a] = stat
        peaks[slot] = stat

    def combine(ref):
        both = [ref[k] for k in range(8)]
        top = both[0][0:4]
        for b in both[1:]:
            top = jnp.maximum(top, b[0:4])
        total = jnp.zeros_like(top)
        for b in both:
            total = total + b[4:8] * jnp.exp(b[0:4] - top)
        return top, total

    def add(low, count, e_ref, e_low, weight, features, squared):
        for at in range(0, count, 128):
            r = (e_ref[pl.ds(e_low + at, 128), :] * weight).astype(BF16)
            resp[pl.ds(at, 128), :] = r
            wide = r.astype(F32)
            mass[pl.ds(low + at, 128), :] += wide[:, 0:128] + wide[:, 128:256] + wide[:, 256:384] + wide[:, 384:512]
        r = resp[pl.ds(0, count), :]
        into = pl.ds(low, count)
        for n in range(4):
            xs = jnp.concatenate([features(2 * n), features(2 * n + 1)], axis=1)
            moments[into, n * 256:(n + 1) * 256] += lax.dot_general(r, xs, CONTRACT, preferred_element_type=F32)
            sq = squared(n)
            moments[into, 1024 + n * 256:1024 + (n + 1) * 256] += lax.dot_general(r, sq, CONTRACT, preferred_element_type=F32)

    def second_round(s):
        arrived(stat_a.at[s, pl.ds(0, 7)], recv_a.at[s])
        top, total = combine(stat_a.at[s])
        stat_b[s, slot_b] = jnp.concatenate([top, total], axis=0)
        for k in range(1, 8):
            push(stat_b.at[s, slot_b], peer_b(k), send_b.at[s], recv_b.at[s])

    def weigh(s):
        arrived(stat_b.at[s, pl.ds(0, 7)], recv_b.at[s])
        top, total = combine(stat_b.at[s])
        log_total = top + jnp.log(total)
        mask = masks[s][0:1, :]
        scale = jnp.exp(peaks[s][0:4] - log_total)
        scale = jnp.concatenate([scale[k:k + 1, :] for k in range(4)], axis=1) * mask
        score = jnp.concatenate([log_total[k:k + 1, :] for k in range(4)], axis=1) * mask
        score_acc[0:1, :] += score
        scales[s] = jnp.broadcast_to(scale, (8, 512))

    def add_chunk(s, low, high=512):
        chunk = grid.at[s // 4, (s // 2) % 2, s % 2]
        add(low, high - low, expo.at[s], low, scales[s][0:1, :], lambda f: chunk[f // 4, f % 4],
            lambda n: squares[s, :, n * 256:(n + 1) * 256])

    @pl.loop(0, CHUNKS + LAG_L)
    def _(it):
        @pl.when(it < CHUNKS)
        def _():
            s = it

            @pl.when(s + AHEAD == 4)
            def _():
                second_here(1)

            arrived(blocks(4, 512), recv_hop.at[s])
            for par in range(2):
                @pl.when((s % 2 == par) & (s < CHUNKS - 1))
                def _():
                    forward(s, par)

                @pl.when(((s + AHEAD) % 2 == par) & (s + AHEAD < CHUNKS))
                def _():
                    hop(s + AHEAD, par)

            @pl.when(s == CHUNKS - 2)
            def _():
                for axis, ref in third(CHUNKS - 1, 1, 0):
                    push(ref, along(axis, 2), send_far.at[0], recv_far.at[0])

        @pl.when(it >= LAG_A)
        def _():
            second_round(it - LAG_A)

        @pl.when((it >= LAG_L) & (it < CHUNKS + LAG_L))
        def _():
            s = it - LAG_L
            @pl.when(s < CHUNKS - 1)
            def _():
                arrived(blocks(2, 512), recv_fwd.at[s])

            @pl.when(s == CHUNKS - 1)
            def _():
                arrived(blocks(2, 512), recv_far.at[0])

            logits_of(s)
            for k in range(1, 8):
                push(stat_a.at[s, slot_a], peer_a(k), send_a.at[s], recv_a.at[s])

            @pl.when(s >= CHUNKS - SHARED)
            def _():
                k = s - (CHUNKS - SHARED)
                for xx in range(2):
                    push(grid.at[s // 4, (s // 2) % 2, s % 2, xx], sibling, send_rows.at[k], recv_rows.at[k], dst=far_rows.at[k, pl.ds(4 * xx, 4)])
                push(squares.at[s], sibling, send_squares.at[k], recv_squares.at[k], dst=far_squares.at[k])
                push(expo.at[s, pl.ds(0, 256)], sibling, send_expo.at[k], recv_expo.at[k], dst=far_expo.at[k])

    @pl.loop(0, CHUNKS - SHARED - 1)
    def _(s):
        due = jnp.where(s == ROUNDS[0], 4, jnp.where(s == ROUNDS[1], 5, jnp.where(s == ROUNDS[2], 6, jnp.where(s == ROUNDS[3], 7, 0))))

        @pl.when(due > 0)
        def _():
            second_round(due)

        weigh(s)
        add_chunk(s, 0)

    weigh(CHUNKS - SHARED - 1)
    add_chunk(CHUNKS - SHARED - 1, 0, 256)
    push(moments.at[pl.ds(0, 256)], sibling, send_one.at[11], recv_one.at[11], dst=got_moments)
    push(mass.at[pl.ds(0, 256)], sibling, send_one.at[12], recv_one.at[12], dst=got_mass)
    add_chunk(CHUNKS - SHARED - 1, 256)

    sent(give, send_one.at[0])
    for part_no in range(3):
        sent(first_done[part_no], send_one.at[1 + part_no])
    for k in range(1, 4):
        sent(second_one, send_x.at[k])
    for group in range(2):
        sent(second_done, send_two.at[1, group])
        sent(second_done, send_two.at[2, group])
    sent(weights.at[1], send_one.at[7])
    sent(offsets.at[1], send_one.at[8])
    sent(valids.at[0, pl.ds(0, 3)], send_one.at[9])
    sent(valids.at[0], send_one.at[10])
    sent(blocks(2, 512), send_far.at[0])

    @pl.loop(0, CHUNKS)
    def _(s):
        sent(blocks(4, 512), send_hop.at[s])
        sent(stat_a.at[s, pl.ds(0, 7)], send_a.at[s])

        @pl.when(s < CHUNKS - 1)
        def _():
            sent(blocks(2, 512), send_fwd.at[s])

    @pl.loop(0, SHARED)
    def _(k):
        s = CHUNKS - SHARED + k
        weigh(s)
        push(scales.at[s], sibling, send_scale.at[k], recv_scale.at[k], dst=far_scale.at[k])

        @pl.when(k == SHARED - 1)
        def _():
            score_plane = jnp.sum(score_acc[0:1, :], axis=1, keepdims=True)
            score_mine[...] = jnp.concatenate([jnp.broadcast_to(score_plane, (4, LANES)), jnp.broadcast_to(count_plane, (4, LANES))], axis=0)
            push(score_mine, sibling, send_one.at[13], recv_one.at[13], dst=score_got)

        add_chunk(s, 256)
        arrived(far_rows.at[k], recv_rows.at[k])
        arrived(far_squares.at[k], recv_squares.at[k])
        arrived(far_expo.at[k], recv_expo.at[k])
        arrived(far_scale.at[k], recv_scale.at[k])
        add(256, 256, far_expo.at[k], 0, far_scale[k][0:1, :], lambda f: far_rows[k, f],
            lambda n: far_squares[k, :, n * 256:(n + 1) * 256])

    arrived(score_got, recv_one.at[13])
    arrived(got_mass, recv_one.at[12])
    arrived(got_moments, recv_one.at[11])

    sent(got_moments, send_one.at[11])
    sent(got_mass, send_one.at[12])
    sent(score_mine, send_one.at[13])
    for k in range(SHARED):
        sent(far_rows.at[k], send_rows.at[k])
        sent(far_squares.at[k], send_squares.at[k])
        sent(far_expo.at[k], send_expo.at[k])
        sent(far_scale.at[k], send_scale.at[k])

    @pl.loop(0, CHUNKS)
    def _(s):
        sent(stat_b.at[s, pl.ds(0, 7)], send_b.at[s])


def finish(moments, got_moments, mass, got_mass, means, prec, score_mine, score_got,
           out_means, out_vars, out_weights, out_score, stage_means, stage_vars, means_sem, vars_sem):
    both = score_mine[...] + score_got[...]
    count = jnp.maximum(both[4:5, 0:1], 1.0)
    out_score[...] = both[0:1, :] / count
    copies = []
    for block in range(4):
        weights = []
        for tile in range(2):
            rows = pl.ds(block * 64 + tile * 32, 32)
            own = pl.ds(256 + block * 64 + tile * 32, 32)
            weight = jnp.sum(mass[own, :] + got_mass[rows, :], axis=1, keepdims=True)
            weights.append(jnp.broadcast_to(weight, (32, LANES)))
            scale = 1.0 / (weight + PRIOR_MASS)
            c = means[rows, :].astype(F32)
            p = prec[rows, :].astype(F32)
            m = (moments[own, 0:1024] + got_moments[rows, 0:1024] + PRIOR_MASS * c) * scale
            stage_means[rows, :] = m
            second = moments[own, 1024:2048] + got_moments[rows, 1024:2048]
            stage_vars[rows, :] = (second + PRIOR_MASS * (1.0 / p + c * c)) * scale - m * m
        rows = pl.ds(block * 64, 64)
        copies.append(pltpu.make_async_copy(stage_means.at[rows], out_means.at[rows], means_sem.at[block]))
        copies.append(pltpu.make_async_copy(stage_vars.at[rows], out_vars.at[rows], vars_sem.at[block]))
        copies[-2].start()
        copies[-1].start()
        weights = jnp.concatenate(weights + weights, axis=0)
        out_weights[block // 2:block // 2 + 1, (block % 2) * 64:(block % 2) * 64 + 64] = jnp.transpose(weights)[0:1, 0:64] / count
    for copy in copies:
        copy.wait()


def functools_sum(items):
    total = items[0]
    for item in items[1:]:
        total = total + item
    return total


def per_device(embeddings, means, precisions, log_weights, valid):
    hbm = pl.BlockSpec(memory_space=pltpu.HBM)
    vmem = pl.BlockSpec(memory_space=pltpu.VMEM)
    dma = pltpu.SemaphoreType.DMA
    found = pl.pallas_call(
        kernel,
        out_shape=(
            pltpu.VMEM((512, 2048), F32),
            pltpu.VMEM((256, 2048), F32),
            pltpu.VMEM((512, LANES), F32),
            pltpu.VMEM((256, LANES), F32),
            pltpu.VMEM((256, 1024), BF16),
            pltpu.VMEM((256, 1024), BF16),
            pltpu.VMEM((8, LANES), F32),
            pltpu.VMEM((8, LANES), F32),
        ),
        in_specs=[hbm] * 5,
        out_specs=[vmem] * 8,
        scratch_shapes=[
            pltpu.VMEM((64, 1024), BF16),
            pltpu.VMEM((16, LANES), F32),
            pltpu.VMEM((8, LANES), jnp.int32),
            pltpu.VMEM((64, 512), BF16),
            pltpu.VMEM((2, 2, 2, 2, 4, 512, LANES), BF16),
            pltpu.VMEM((2, 256, 2048), BF16),
            pltpu.VMEM((2, 256, LANES), F32),
            pltpu.VMEM((2, 4, 8, LANES), F32),
            pltpu.VMEM((CHUNKS, 8, 512), F32),
            pltpu.VMEM((CHUNKS, 512, 1024), BF16),
            pltpu.VMEM((CHUNKS, 512, 512), F32),
            pltpu.VMEM((CHUNKS, 8, LANES), F32),
            pltpu.VMEM((CHUNKS, 8, 8, LANES), F32),
            pltpu.VMEM((CHUNKS, 8, 8, LANES), F32),
            pltpu.VMEM((512, 512), BF16),
            pltpu.VMEM((SHARED, 8, 512, LANES), BF16),
            pltpu.VMEM((SHARED, 512, 1024), BF16),
            pltpu.VMEM((SHARED, 256, 512), F32),
            pltpu.VMEM((CHUNKS, 8, 512), F32),
            pltpu.VMEM((SHARED, 8, 512), F32),
            pltpu.VMEM((8, 512), F32),
            dma((5,)),
            dma((17,)), dma((17,)),
            dma((3, 2)), dma((3, 2)),
            dma((4,)), dma((4,)),
            dma((SHARED,)), dma((SHARED,)), dma((SHARED,)), dma((SHARED,)),
            dma((SHARED,)), dma((SHARED,)), dma((SHARED,)), dma((SHARED,)),
            dma((1,)), dma((1,)),
            dma((CHUNKS,)), dma((CHUNKS,)),
            dma((CHUNKS,)), dma((CHUNKS,)),
            dma((CHUNKS,)), dma((CHUNKS,)),
            dma((CHUNKS,)), dma((CHUNKS,)),
        ],
        compiler_params=pltpu.CompilerParams(
            collective_id=0, has_side_effects=True, vmem_limit_bytes=50 << 20
        ),
        cost_estimate=pl.CostEstimate(flops=17 << 30, bytes_accessed=8 << 20, transcendentals=4 << 20),
        name="mixture_step",
    )(embeddings.T, means, precisions, log_weights.reshape(16, LANES), valid.reshape(8, LANES))
    found = [pltpu.with_memory_space_constraint(a, pltpu.VMEM) for a in found]
    new_means, new_vars, weights, score = pl.pallas_call(
        finish,
        out_shape=(
            jax.ShapeDtypeStruct((256, 1024), F32),
            jax.ShapeDtypeStruct((256, 1024), F32),
            jax.ShapeDtypeStruct((2, LANES), F32),
            jax.ShapeDtypeStruct((1, LANES), F32),
        ),
        in_specs=[vmem] * 8,
        out_specs=[hbm, hbm, vmem, vmem],
        scratch_shapes=[pltpu.VMEM((256, 1024), F32), pltpu.VMEM((256, 1024), F32), dma((4,)), dma((4,))],
        compiler_params=pltpu.CompilerParams(vmem_limit_bytes=8 << 20),
        cost_estimate=pl.CostEstimate(flops=4 << 20, bytes_accessed=2 << 20, transcendentals=0),
        name="new_parameters",
    )(*found)
    return new_means, new_vars, weights.reshape(256), score[0, 0]


def solution(mesh):
    in_specs = (P("dp", "comp"), P("comp", None), P("comp", None), P("comp"), P("dp"))
    out_specs = (P(("comp", "dp"), None), P(("comp", "dp"), None), P(("comp", "dp")), P())
    return jax.shard_map(
        per_device, mesh=mesh, in_specs=in_specs, out_specs=out_specs, check_vma=False
    )
```

```python
import math

import jax
import jax.numpy as jnp
from jax import lax
from jax.sharding import PartitionSpec as P
import jax.experimental.pallas as pl
import jax.experimental.pallas.tpu as pltpu

PRIOR_MASS = 1.0
MESH = pl.DeviceIdType.MESH
F32, BF16 = jnp.float32, jnp.bfloat16

SIZE = ((32, 96, 96), (48, 80, 80))
BASE = ((0, 128, 320), (0, 192, 352))
FROM_0, FROM_1, FROM_2 = (0, 32, 80, 112), (160, 256), (336, 432)
CHUNKS = 8
AHEAD = 3
SHARED = 1
ROUNDS = (0, 1, 2, 4)
LAG_L, LAG_A = 3, 7
LANES = 128
CONTRACT_LAST = (((1,), (1,)), ((), ()))
CONTRACT = (((1,), (0,)), ((), ()))


def kernel(emb_hbm, means_hbm, prec_hbm, lw_hbm, valid_hbm,
           moments, got_moments, mass, got_mass, means, prec, score_mine, score_got,
           emb, lw_ref, valid_ref, take, grid, weights, offsets, valids, masks,
           squares, expo, peaks, stat_a, stat_b, resp, far_rows, far_squares, far_expo, scales, far_scale, score_acc,
           load_sem, send_one, recv_one, send_two, recv_two, send_x, recv_x, send_rows, recv_rows, send_squares, recv_squares, send_expo, recv_expo, send_scale, recv_scale, send_far, recv_far, send_hop, recv_hop, send_fwd, recv_fwd, send_a, recv_a, send_b, recv_b):
    dp, comp = lax.axis_index("dp"), lax.axis_index("comp")
    xh, y = dp // 4, dp % 4
    xl, z, core = comp // 8, (comp // 2) % 4, comp % 2
    x = xh * 2 + xl
    temper = 0.5 * math.sqrt(1024)

    def dev(x, y, z, core):
        return ((x // 2) * 4 + y, (x % 2) * 8 + z * 2 + core)

    def along(axis, step):
        if axis == "x":
            return dev((x + step) % 4, y, z, core)
        if axis == "y":
            return dev(x, (y + step) % 4, z, core)
        return dev(x, y, (z + step) % 4, core)

    sibling = dev(x, y, z, 1 - core)
    slot_a = x * 2 + y % 2
    slot_b = z * 2 + y // 2

    def peer_a(k):
        to = (slot_a + k) % 8
        return dev(to // 2, (y // 2) * 2 + to % 2, z, core)

    def peer_b(k):
        to = (slot_b + k) % 8
        return dev(x, (to % 2) * 2 + y % 2, to // 2, core)

    def push(ref, to, ssem, rsem, dst=None):
        pltpu.make_async_remote_copy(
            src_ref=ref, dst_ref=ref if dst is None else dst, send_sem=ssem, recv_sem=rsem, device_id=to, device_id_type=MESH
        ).start()

    def arrived(ref, rsem):
        pltpu.make_async_remote_copy(
            src_ref=ref, dst_ref=ref, send_sem=send_one.at[0], recv_sem=rsem, device_id=sibling, device_id_type=MESH
        ).wait_recv()

    def sent(ref, ssem):
        pltpu.make_async_remote_copy(
            src_ref=ref, dst_ref=ref, send_sem=ssem, recv_sem=recv_one.at[0], device_id=sibling, device_id_type=MESH
        ).wait_send()

    own = pl.multiple_of(dp * 256, 256)
    load_emb = pltpu.make_async_copy(emb_hbm, emb, load_sem.at[0])
    load_means = pltpu.make_async_copy(means_hbm.at[pl.ds(own, 256)], means, load_sem.at[1])
    load_prec = pltpu.make_async_copy(prec_hbm.at[pl.ds(own, 256)], prec, load_sem.at[2])
    load_lw = pltpu.make_async_copy(lw_hbm, lw_ref, load_sem.at[3])
    load_valid = pltpu.make_async_copy(valid_hbm, valid_ref, load_sem.at[4])
    load_emb.start()
    load_valid.start()
    load_lw.start()
    load_means.start()
    load_prec.start()

    barrier = pltpu.get_barrier_semaphore()
    friends = [sibling]
    for k in range(1, 4):
        friends += [along("x", k), along("y", k), along("z", k)]
        friends += []
    for k in range(4):
        if k:
            friends.append(dev((x + k) % 4, (y // 2) * 2 + 1 - y % 2, z, core))
            friends.append(dev(x, (y + 2) % 4, (z + k) % 4, core))
    for friend in friends:
        pl.semaphore_signal(barrier, inc=1, device_id=friend, device_id_type=MESH)
    pl.semaphore_wait(barrier, len(friends))

    load_emb.wait()
    give = emb.at[:, pl.ds(pl.multiple_of((1 - core) * 512, 512), 512)]
    push(give, sibling, send_one.at[0], recv_one.at[0], dst=take)
    load_valid.wait()
    vrow = jnp.where(core == 0, valid_ref[0:4, :], valid_ref[4:8, :]).astype(F32)
    valids[xh, y] = jnp.concatenate([vrow, vrow], axis=0)
    for k in range(1, 4):
        push(valids.at[xh, y], along("y", k), send_one.at[9], recv_one.at[9])
    kept = emb[:, pl.ds(pl.multiple_of(core * 512, 512), 512)]
    arrived(take, recv_one.at[0])
    taken = take[...]
    shard = jnp.concatenate([jnp.where(core == 0, kept, taken), jnp.where(core == 0, taken, kept)], axis=0)
    shard = jnp.transpose(shard)
    def rows_of(part, par, index):
        n = SIZE[par][part]
        return pl.ds(pl.multiple_of(BASE[par][part] + index * n, 16), n)

    for par in range(2):
        for jh in range(2):
            at = FROM_0[2 * jh + par]
            grid[xh, jh, par, xl, z, rows_of(0, par, y), :] = shard[at:at + SIZE[par][0]]
        at = FROM_1[par]
        grid[xh, y // 2, par, xl, z, rows_of(1, par, y % 2), :] = shard[at:at + SIZE[par][1]]
        at = FROM_2[par]
        grid[y // 2, y % 2, par, xl, z, rows_of(2, par, xh), :] = shard[at:at + SIZE[par][2]]

    first = []
    for par in range(2):
        first += [
            (0, "z", grid.at[xh, :, par, xl, z, rows_of(0, par, y)]),
            (1, "x", grid.at[xh, y // 2, par, xl, z, rows_of(1, par, y % 2)]),
            (2, "y", grid.at[y // 2, y % 2, par, xl, z, rows_of(2, par, xh)]),
        ]
    for k in range(1, 4):
        for part_no, axis, ref in first:
            push(ref, along(axis, k), send_one.at[1 + part_no], recv_one.at[1 + part_no])

    for par in range(2):
        for k in range(1, 4):
            push(grid.at[xh, :, par, xl, z, rows_of(0, par, y)], along("x", k), send_x.at[k], recv_x.at[k])
            push(grid.at[xh, y // 2, par, xl, z, rows_of(1, par, y % 2)], along("y", k), send_two.at[1, xh], recv_two.at[1, xh])
            push(grid.at[y // 2, y % 2, par, xl, z, rows_of(2, par, xh)], along("z", k), send_two.at[2, y // 2], recv_two.at[2, y // 2])

    load_means.wait()
    load_prec.wait()
    load_lw.wait()
    for tile in range(2):
        row = jnp.broadcast_to(lw_ref[pl.ds(dp * 2 + tile, 1), :], (LANES, LANES))
        offsets[1, tile * LANES:(tile + 1) * LANES, :] = jnp.transpose(row)

    @pl.loop(0, 8)
    def _(t):
        rows = pl.ds(pl.multiple_of(t * 32, 32), 32)
        p = prec[rows, :].astype(F32)
        c = means[rows, :].astype(F32)
        scaled = (p * c).astype(BF16).astype(F32)
        halfp = (0.5 * p).astype(BF16).astype(F32)
        weights[1, rows, 0:1024] = (scaled * (1.0 / temper)).astype(BF16)
        weights[1, rows, 1024:2048] = (halfp * (-1.0 / temper)).astype(BF16)
        both = 0.5 * jnp.sum(jnp.log(p), axis=1, keepdims=True) - 0.5 * jnp.sum(p * c * c, axis=1, keepdims=True)
        offsets[1, rows, :] = (offsets[1, rows, :] + both) * (1.0 / temper)

    push(weights.at[1], sibling, send_one.at[7], recv_one.at[7], dst=weights.at[0])
    push(offsets.at[1], sibling, send_one.at[8], recv_one.at[8], dst=offsets.at[0])

    def blocks(n, rows):
        return grid.at[0, 0, 0, pl.ds(0, n // 4), :, pl.ds(0, rows)] if n % 4 == 0 else grid.at[0, 0, 0, 0, pl.ds(0, n), pl.ds(0, rows)]

    first_done = (blocks(3, 160), blocks(3, 176), blocks(3, 176))
    second_one = blocks(4, 160)
    second_done = blocks(3, 352)

    def second(part_no, group):
        def copies(select):
            for par in range(2):
                for k in range(1, 4):
                    if part_no == 1:
                        push(grid.at[group, y // 2, par, select(xl), z, rows_of(1, par, y % 2)], along("y", k), send_two.at[1, group], recv_two.at[1, group])
                    else:
                        push(grid.at[group, select(y % 2), par, xl, z, rows_of(2, par, xh)], along("z", k), send_two.at[2, group], recv_two.at[2, group])

        mine = xh if part_no == 1 else y // 2

        @pl.when(mine == group)
        def _():
            copies(lambda own: 1 - own)

        @pl.when(mine != group)
        def _():
            copies(lambda own: slice(None))

    def second_rows():
        for par in range(2):
            for k in range(1, 4):
                for other in range(1, 4):
                    push(grid.at[xh, :, par, xl, (z + other) % 4, rows_of(0, par, y)], along("x", k), send_x.at[k], recv_x.at[k])

    def second_here(group):
        for k in range(1, 4):
            @pl.when(((x + 4 - k) % 4) // 2 == group)
            def _():
                arrived(second_one, recv_x.at[k])

        arrived(second_done, recv_two.at[1, group])
        arrived(second_done, recv_two.at[2, group])

    arrived(first_done[0], recv_one.at[1])
    second_rows()
    for part_no in (1, 2):
        arrived(first_done[part_no], recv_one.at[1 + part_no])
        second(part_no, 0)
    for part_no in (1, 2):
        second(part_no, 1)
    arrived(valids.at[0, pl.ds(0, 3)], recv_one.at[9])
    push(valids.at[xh], along("x", 2), send_one.at[10], recv_one.at[10])

    moments[...] = jnp.zeros_like(moments)
    mass[...] = jnp.zeros_like(mass)
    score_acc[...] = jnp.zeros_like(score_acc)

    def third(s, par, step):
        i, jh = s // 4, (s // 2) % 2
        yy, zz, xx = (y + step) % 4, (z + step) % 4, (x + step) % 4
        return (
            ("y", grid.at[i, jh, par, :, :, rows_of(0, par, yy)]),
            ("z", grid.at[i, jh, par, :, zz, pl.ds(BASE[par][1], 2 * SIZE[par][1])]),
            ("x", grid.at[i, jh, par, xx % 2, :, rows_of(2, par, xx // 2)]),
        )

    def hop(s, par):
        for axis, ref in third(s, par, 0):
            for step in (1, 3):
                push(ref, along(axis, step), send_hop.at[s], recv_hop.at[s])

    def forward(s, par):
        i, jh = s // 4, (s // 2) % 2
        for half, step in ((0, 1), (1, 3)):
            yy, zz, xx = (y + 4 - step) % 4, (z + 4 - step) % 4, (x + 4 - step) % 4
            for axis, ref in (
                ("y", grid.at[i, jh, par, half, :, rows_of(0, par, yy)]),
                ("z", grid.at[i, jh, par, half, zz, pl.ds(BASE[par][1], 2 * SIZE[par][1])]),
                ("x", grid.at[i, jh, par, xx % 2, pl.ds(2 * half, 2), rows_of(2, par, xx // 2)]),
            ):
                push(ref, along(axis, step), send_fwd.at[s], recv_fwd.at[s])

    second_here(0)
    for s in range(AHEAD):
        hop(s, s % 2)

    arrived(valids.at[0], recv_one.at[10])
    place = lax.broadcasted_iota(jnp.int32, (8, 512), 1)

    def lanes_of(block):
        v = valids[block // 4, block % 4]
        return jnp.broadcast_to(jnp.concatenate([v[i:i + 1, :] for i in range(4)], axis=1), (8, 512))

    by_block = [lanes_of(b) for b in range(8)]
    count_plane = functools_sum([jnp.sum(b[0:1, :], axis=1, keepdims=True) for b in by_block])
    for s in range(CHUNKS):
        par = s % 2
        n0, n1, n2 = SIZE[par]
        b0, b1, b2 = BASE[par]
        out = by_block[s]
        for yy in range(4):
            moved = pltpu.roll(by_block[(s // 4) * 4 + yy], (yy * n0 - FROM_0[s % 4]) % 512, 1)
            out = jnp.where((place >= yy * n0) & (place < (yy + 1) * n0), moved, out)
        for k in range(2):
            at = b1 + k * n1
            moved = pltpu.roll(by_block[(s // 2) * 2 + k], (at - FROM_1[par]) % 512, 1)
            out = jnp.where((place >= at) & (place < at + n1), moved, out)
            at = b2 + k * n2
            moved = pltpu.roll(by_block[k * 4 + s // 2], (at - FROM_2[par]) % 512, 1)
            out = jnp.where((place >= at) & (place < at + n2), moved, out)
        masks[s] = out

    arrived(weights.at[0], recv_one.at[7])
    arrived(offsets.at[0], recv_one.at[8])

    def logits_of(s):
        chunk, slot = grid.at[s // 4, (s // 2) % 2, s % 2], s
        tops, sums = [], []
        for n in range(2):
            rows = pl.ds(n * 256, 256)
            xs = jnp.concatenate([chunk[f // 4, f % 4, rows, :] for f in range(8)], axis=1)
            wide = xs.astype(F32)
            sq = (wide * wide).astype(BF16)
            squares[slot, rows, :] = sq
            w = weights[...].reshape(512, 2048)
            l = lax.dot_general(w[:, 0:1024], xs, CONTRACT_LAST, preferred_element_type=F32)
            l = l + lax.dot_general(w[:, 1024:2048], sq, CONTRACT_LAST, preferred_element_type=F32)
            off = offsets[...].reshape(512, LANES)
            l = l + jnp.concatenate([off, off], axis=1)
            top = jnp.max(l, axis=0, keepdims=True)
            e = jnp.exp(l - top)
            expo[slot, :, rows] = e
            total = jnp.sum(e, axis=0, keepdims=True)
            tops += [top[:, 0:128], top[:, 128:256]]
            sums += [total[:, 0:128], total[:, 128:256]]
        stat = jnp.concatenate(tops + sums, axis=0)
        stat_a[s, slot_a] = stat
        peaks[slot] = stat

    def combine(ref):
        both = [ref[k] for k in range(8)]
        top = both[0][0:4]
        for b in both[1:]:
            top = jnp.maximum(top, b[0:4])
        total = jnp.zeros_like(top)
        for b in both:
            total = total + b[4:8] * jnp.exp(b[0:4] - top)
        return top, total

    def add(low, count, e_ref, e_low, weight, features, squared, between=lambda: None):
        for at in range(0, count, 128):
            r = (e_ref[pl.ds(e_low + at, 128), :] * weight).astype(BF16)
            resp[pl.ds(at, 128), :] = r
            wide = r.astype(F32)
            mass[pl.ds(low + at, 128), :] += wide[:, 0:128] + wide[:, 128:256] + wide[:, 256:384] + wide[:, 384:512]
        r = resp[pl.ds(0, count), :]
        into = pl.ds(low, count)
        for n in range(4):
            xs = jnp.concatenate([features(2 * n), features(2 * n + 1)], axis=1)
            moments[into, n * 256:(n + 1) * 256] += lax.dot_general(r, xs, CONTRACT, preferred_element_type=F32)
        between()
        for n in range(4):
            sq = squared(n)
            moments[into, 1024 + n * 256:1024 + (n + 1) * 256] += lax.dot_general(r, sq, CONTRACT, preferred_element_type=F32)

    def second_round(s):
        arrived(stat_a.at[s, pl.ds(0, 7)], recv_a.at[s])
        top, total = combine(stat_a.at[s])
        stat_b[s, slot_b] = jnp.concatenate([top, total], axis=0)
        for k in range(1, 8):
            push(stat_b.at[s, slot_b], peer_b(k), send_b.at[s], recv_b.at[s])

    def weigh(s):
        arrived(stat_b.at[s, pl.ds(0, 7)], recv_b.at[s])
        top, total = combine(stat_b.at[s])
        log_total = top + jnp.log(total)
        mask = masks[s][0:1, :]
        scale = jnp.exp(peaks[s][0:4] - log_total)
        scale = jnp.concatenate([scale[k:k + 1, :] for k in range(4)], axis=1) * mask
        score = jnp.concatenate([log_total[k:k + 1, :] for k in range(4)], axis=1) * mask
        score_acc[0:1, :] += score
        scales[s] = jnp.broadcast_to(scale, (8, 512))

    def add_chunk(s, low, high=512, between=lambda: None):
        chunk = grid.at[s // 4, (s // 2) % 2, s % 2]
        add(low, high - low, expo.at[s], low, scales[s][0:1, :], lambda f: chunk[f // 4, f % 4],
            lambda n: squares[s, :, n * 256:(n + 1) * 256], between)

    @pl.loop(0, CHUNKS + LAG_L)
    def _(it):
        @pl.when(it < CHUNKS)
        def _():
            s = it

            @pl.when(s + AHEAD == 4)
            def _():
                second_here(1)

            arrived(blocks(4, 512), recv_hop.at[s])
            for par in range(2):
                @pl.when((s % 2 == par) & (s < CHUNKS - 1))
                def _():
                    forward(s, par)

                @pl.when(((s + AHEAD) % 2 == par) & (s + AHEAD < CHUNKS))
                def _():
                    hop(s + AHEAD, par)

            @pl.when(s == CHUNKS - 2)
            def _():
                for axis, ref in third(CHUNKS - 1, 1, 0):
                    push(ref, along(axis, 2), send_far.at[0], recv_far.at[0])

        @pl.when(it >= LAG_A)
        def _():
            second_round(it - LAG_A)

        @pl.when((it >= LAG_L) & (it < CHUNKS + LAG_L))
        def _():
            s = it - LAG_L
            @pl.when(s < CHUNKS - 1)
            def _():
                arrived(blocks(2, 512), recv_fwd.at[s])

            @pl.when(s == CHUNKS - 1)
            def _():
                arrived(blocks(2, 512), recv_far.at[0])

            logits_of(s)
            for k in range(1, 8):
                push(stat_a.at[s, slot_a], peer_a(k), send_a.at[s], recv_a.at[s])

            @pl.when(s >= CHUNKS - SHARED)
            def _():
                k = s - (CHUNKS - SHARED)
                for xx in range(2):
                    push(grid.at[s // 4, (s // 2) % 2, s % 2, xx], sibling, send_rows.at[k], recv_rows.at[k], dst=far_rows.at[k, pl.ds(4 * xx, 4)])
                push(squares.at[s], sibling, send_squares.at[k], recv_squares.at[k], dst=far_squares.at[k])
                push(expo.at[s, pl.ds(0, 256)], sibling, send_expo.at[k], recv_expo.at[k], dst=far_expo.at[k])

    @pl.loop(0, CHUNKS - SHARED - 1)
    def _(s):
        due = jnp.where(s == ROUNDS[0], 4, jnp.where(s == ROUNDS[1], 5, jnp.where(s == ROUNDS[2], 6, jnp.where(s == ROUNDS[3], 7, 0))))

        @pl.when(due > 0)
        def _():
            second_round(due)

        weigh(s)
        add_chunk(s, 0)

    weigh(CHUNKS - SHARED - 1)
    def send_moments(column, sem):
        columns = pl.ds(column, 1024)
        push(moments.at[pl.ds(0, 256), columns], sibling, send_one.at[sem], recv_one.at[sem], dst=got_moments.at[:, columns])

    add_chunk(CHUNKS - SHARED - 1, 0, 256, lambda: send_moments(0, 11))
    send_moments(1024, 14)
    push(mass.at[pl.ds(0, 256)], sibling, send_one.at[12], recv_one.at[12], dst=got_mass)
    add_chunk(CHUNKS - SHARED - 1, 256)

    sent(give, send_one.at[0])
    for part_no in range(3):
        sent(first_done[part_no], send_one.at[1 + part_no])
    for k in range(1, 4):
        sent(second_one, send_x.at[k])
    for group in range(2):
        sent(second_done, send_two.at[1, group])
        sent(second_done, send_two.at[2, group])
    sent(weights.at[1], send_one.at[7])
    sent(offsets.at[1], send_one.at[8])
    sent(valids.at[0, pl.ds(0, 3)], send_one.at[9])
    sent(valids.at[0], send_one.at[10])
    sent(blocks(2, 512), send_far.at[0])

    @pl.loop(0, CHUNKS)
    def _(s):
        sent(blocks(4, 512), send_hop.at[s])
        sent(stat_a.at[s, pl.ds(0, 7)], send_a.at[s])

        @pl.when(s < CHUNKS - 1)
        def _():
            sent(blocks(2, 512), send_fwd.at[s])

    @pl.loop(0, SHARED)
    def _(k):
        s = CHUNKS - SHARED + k
        weigh(s)
        push(scales.at[s], sibling, send_scale.at[k], recv_scale.at[k], dst=far_scale.at[k])

        @pl.when(k == SHARED - 1)
        def _():
            score_plane = jnp.sum(score_acc[0:1, :], axis=1, keepdims=True)
            score_mine[...] = jnp.concatenate([jnp.broadcast_to(score_plane, (4, LANES)), jnp.broadcast_to(count_plane, (4, LANES))], axis=0)
            push(score_mine, sibling, send_one.at[13], recv_one.at[13], dst=score_got)

        add_chunk(s, 256)
        arrived(far_rows.at[k], recv_rows.at[k])
        arrived(far_squares.at[k], recv_squares.at[k])
        arrived(far_expo.at[k], recv_expo.at[k])
        arrived(far_scale.at[k], recv_scale.at[k])
        add(256, 256, far_expo.at[k], 0, far_scale[k][0:1, :], lambda f: far_rows[k, f],
            lambda n: far_squares[k, :, n * 256:(n + 1) * 256])

    arrived(score_got, recv_one.at[13])
    arrived(got_mass, recv_one.at[12])
    arrived(got_moments.at[:, pl.ds(0, 1024)], recv_one.at[11])
    arrived(got_moments.at[:, pl.ds(1024, 1024)], recv_one.at[14])

    sent(got_moments.at[:, pl.ds(0, 1024)], send_one.at[11])
    sent(got_moments.at[:, pl.ds(1024, 1024)], send_one.at[14])
    sent(got_mass, send_one.at[12])
    sent(score_mine, send_one.at[13])
    for k in range(SHARED):
        sent(far_rows.at[k], send_rows.at[k])
        sent(far_squares.at[k], send_squares.at[k])
        sent(far_expo.at[k], send_expo.at[k])
        sent(far_scale.at[k], send_scale.at[k])

    @pl.loop(0, CHUNKS)
    def _(s):
        sent(stat_b.at[s, pl.ds(0, 7)], send_b.at[s])


def finish(moments, got_moments, mass, got_mass, means, prec, score_mine, score_got,
           out_means, out_vars, out_weights, out_score, stage_means, stage_vars, means_sem, vars_sem):
    both = score_mine[...] + score_got[...]
    count = jnp.maximum(both[4:5, 0:1], 1.0)
    out_score[...] = both[0:1, :] / count
    copies = []
    for block in range(4):
        weights = []
        for tile in range(2):
            rows = pl.ds(block * 64 + tile * 32, 32)
            own = pl.ds(256 + block * 64 + tile * 32, 32)
            weight = jnp.sum(mass[own, :] + got_mass[rows, :], axis=1, keepdims=True)
            weights.append(jnp.broadcast_to(weight, (32, LANES)))
            scale = 1.0 / (weight + PRIOR_MASS)
            c = means[rows, :].astype(F32)
            p = prec[rows, :].astype(F32)
            m = (moments[own, 0:1024] + got_moments[rows, 0:1024] + PRIOR_MASS * c) * scale
            stage_means[rows, :] = m
            second = moments[own, 1024:2048] + got_moments[rows, 1024:2048]
            stage_vars[rows, :] = (second + PRIOR_MASS * (1.0 / p + c * c)) * scale - m * m
        rows = pl.ds(block * 64, 64)
        copies.append(pltpu.make_async_copy(stage_means.at[rows], out_means.at[rows], means_sem.at[block]))
        copies.append(pltpu.make_async_copy(stage_vars.at[rows], out_vars.at[rows], vars_sem.at[block]))
        copies[-2].start()
        copies[-1].start()
        weights = jnp.concatenate(weights + weights, axis=0)
        out_weights[block // 2:block // 2 + 1, (block % 2) * 64:(block % 2) * 64 + 64] = jnp.transpose(weights)[0:1, 0:64] / count
    for copy in copies:
        copy.wait()


def functools_sum(items):
    total = items[0]
    for item in items[1:]:
        total = total + item
    return total


def per_device(embeddings, means, precisions, log_weights, valid):
    hbm = pl.BlockSpec(memory_space=pltpu.HBM)
    vmem = pl.BlockSpec(memory_space=pltpu.VMEM)
    dma = pltpu.SemaphoreType.DMA
    found = pl.pallas_call(
        kernel,
        out_shape=(
            pltpu.VMEM((512, 2048), F32),
            pltpu.VMEM((256, 2048), F32),
            pltpu.VMEM((512, LANES), F32),
            pltpu.VMEM((256, LANES), F32),
            pltpu.VMEM((256, 1024), BF16),
            pltpu.VMEM((256, 1024), BF16),
            pltpu.VMEM((8, LANES), F32),
            pltpu.VMEM((8, LANES), F32),
        ),
        in_specs=[hbm] * 5,
        out_specs=[vmem] * 8,
        scratch_shapes=[
            pltpu.VMEM((64, 1024), BF16),
            pltpu.VMEM((16, LANES), F32),
            pltpu.VMEM((8, LANES), jnp.int32),
            pltpu.VMEM((64, 512), BF16),
            pltpu.VMEM((2, 2, 2, 2, 4, 512, LANES), BF16),
            pltpu.VMEM((2, 256, 2048), BF16),
            pltpu.VMEM((2, 256, LANES), F32),
            pltpu.VMEM((2, 4, 8, LANES), F32),
            pltpu.VMEM((CHUNKS, 8, 512), F32),
            pltpu.VMEM((CHUNKS, 512, 1024), BF16),
            pltpu.VMEM((CHUNKS, 512, 512), F32),
            pltpu.VMEM((CHUNKS, 8, LANES), F32),
            pltpu.VMEM((CHUNKS, 8, 8, LANES), F32),
            pltpu.VMEM((CHUNKS, 8, 8, LANES), F32),
            pltpu.VMEM((512, 512), BF16),
            pltpu.VMEM((SHARED, 8, 512, LANES), BF16),
            pltpu.VMEM((SHARED, 512, 1024), BF16),
            pltpu.VMEM((SHARED, 256, 512), F32),
            pltpu.VMEM((CHUNKS, 8, 512), F32),
            pltpu.VMEM((SHARED, 8, 512), F32),
            pltpu.VMEM((8, 512), F32),
            dma((5,)),
            dma((17,)), dma((17,)),
            dma((3, 2)), dma((3, 2)),
            dma((4,)), dma((4,)),
            dma((SHARED,)), dma((SHARED,)), dma((SHARED,)), dma((SHARED,)),
            dma((SHARED,)), dma((SHARED,)), dma((SHARED,)), dma((SHARED,)),
            dma((1,)), dma((1,)),
            dma((CHUNKS,)), dma((CHUNKS,)),
            dma((CHUNKS,)), dma((CHUNKS,)),
            dma((CHUNKS,)), dma((CHUNKS,)),
            dma((CHUNKS,)), dma((CHUNKS,)),
        ],
        compiler_params=pltpu.CompilerParams(
            collective_id=0, has_side_effects=True, vmem_limit_bytes=50 << 20
        ),
        cost_estimate=pl.CostEstimate(flops=17 << 30, bytes_accessed=8 << 20, transcendentals=4 << 20),
        name="mixture_step",
    )(embeddings.T, means, precisions, log_weights.reshape(16, LANES), valid.reshape(8, LANES))
    found = [pltpu.with_memory_space_constraint(a, pltpu.VMEM) for a in found]
    new_means, new_vars, weights, score = pl.pallas_call(
        finish,
        out_shape=(
            jax.ShapeDtypeStruct((256, 1024), F32),
            jax.ShapeDtypeStruct((256, 1024), F32),
            jax.ShapeDtypeStruct((2, LANES), F32),
            jax.ShapeDtypeStruct((1, LANES), F32),
        ),
        in_specs=[vmem] * 8,
        out_specs=[hbm, hbm, vmem, vmem],
        scratch_shapes=[pltpu.VMEM((256, 1024), F32), pltpu.VMEM((256, 1024), F32), dma((4,)), dma((4,))],
        compiler_params=pltpu.CompilerParams(vmem_limit_bytes=8 << 20),
        cost_estimate=pl.CostEstimate(flops=4 << 20, bytes_accessed=2 << 20, transcendentals=0),
        name="new_parameters",
    )(*found)
    return new_means, new_vars, weights.reshape(256), score[0, 0]


def solution(mesh):
    in_specs = (P("dp", "comp"), P("comp", None), P("comp", None), P("comp"), P("dp"))
    out_specs = (P(("comp", "dp"), None), P(("comp", "dp"), None), P(("comp", "dp")), P())
    return jax.shard_map(
        per_device, mesh=mesh, in_specs=in_specs, out_specs=out_specs, check_vma=False
    )
```
